512 devices in a mesh: ctx: 32 (over x, z), dp: 16 (over y, core).
Axes of the slice: x: 4, y: 8, z: 8, core: 2. Of those that a mesh axis runs over, the one named last changes fastest.
Arguments:
- queries: bfloat16 [65536, 4096], P(('dp', 'ctx')), parts along dimension 0, may hold values from -5 to 5
- keys: bfloat16 [65536, 512], P(('dp', 'ctx')), parts along dimension 0, may hold values from -5 to 5
- values: bfloat16 [65536, 512], P(('dp', 'ctx')), parts along dimension 0, may hold values from -6 to 6
- output_gradient: bfloat16 [65536, 4096], P(('dp', 'ctx')), parts along dimension 0, may hold values from -6 to 6
- doc_lengths: int32 [336], P('dp'), parts along dimension 0, may hold values from 1 to 384, 4096 in all
- span_order: int32 [1024], P('dp'), parts along dimension 0, may hold values from 0 to 63, each once
Outputs:
- attended: bfloat16 [65536, 4096], P(('dp', 'ctx')), parts along dimension 0
- grad_queries: bfloat16 [65536, 4096], P(('dp', 'ctx')), parts along dimension 0
- grad_keys: bfloat16 [65536, 512], P(('dp', 'ctx')), parts along dimension 0
- grad_values: bfloat16 [65536, 512], P(('dp', 'ctx')), parts along dimension 0
The draws below stay inside these ranges and needn't reach their ends.
There are 16 independent parts, one for each index of `dp`. The reference program is written for one: setup_inputs(seed, part) draws one part's arguments, and reference() takes and returns one part's arrays. A program takes and returns all parts, laid end to end along the dimension named above; each array names one. Nothing has to cross between parts.
Inputs may be any that keep to these rules, and one draw needn't show every extreme that they name: `doc_lengths`: the largest length is exactly 384. `span_order`: a permutation.
All inputs are finite; a program needn't handle non-finite values.
Results may differ from the reference program's by a relative error of at most 0.0071.
Values may be sent and summed in bfloat16 or wider, within the bound.
A program may use at most 64 MiB of HBM per device.

```python
import math
import jax
import jax.numpy as jnp
import numpy as np
from jax import lax

HEAD_DIMENSION = 128
QUERY_HEADS = 32
KEY_VALUE_HEADS = 4
MOST = 384
WINDOW_TOKENS = 4096
NCHUNK = 64
NDOCS = 21
QB = 512


def draw_queries(key, part):
    key = jax.random.fold_in(key, 1)
    drawn_layout = jnp.clip(jax.random.normal(key, (WINDOW_TOKENS, QUERY_HEADS * HEAD_DIMENSION), jnp.float32), -5.0, 5.0)
    return drawn_layout.astype(jnp.bfloat16)


def draw_keys(key, part):
    key = jax.random.fold_in(key, 2)
    drawn_layout = jnp.clip(jax.random.normal(key, (WINDOW_TOKENS, KEY_VALUE_HEADS * HEAD_DIMENSION), jnp.float32), -5.0, 5.0)
    return drawn_layout.astype(jnp.bfloat16)


def block_levels(key, shape, cuts, least, top_value):
    factor_of, own = 1.0, jax.random.fold_in(key, 6)
    for dim, blocks in cuts:
        draws = jnp.exp(jax.random.uniform(jax.random.fold_in(own, dim), (blocks,), jnp.float32, least / len(cuts), top_value / len(cuts)))
        factor_of = factor_of * jnp.repeat(draws, shape[dim] // blocks).reshape([-1 if axis == dim else 1 for axis in range(len(shape))])
    return factor_of


def profile(amount, total, most, slope):
    weights = [(1 << 20) // math.isqrt(standing ** slope) + 1 for standing in range(2, amount + 1)]
    surplus, counts = total - most - (amount - 1), [1] * (amount - 1)
    while surplus > 0:
        free = [i for i in range(amount - 1) if counts[i] < most]
        mass, left = sum([weights[i] for i in free]), surplus
        for i in free:
            addition = min(most - counts[i], max(1, left * weights[i] // mass), surplus)
            counts[i] = counts[i] + addition
            surplus = surplus - addition
    return np.array([most] + counts)


def ragged(key, amount, total, most, lean):
    if amount == 2:
        one = jax.random.randint(key, (), max(1, total - most), min(most, total - 1) + 1)
        return jnp.stack([one, total - one])
    tallies = jnp.asarray(profile(amount, total, most, lean), jnp.int32)
    twos = (amount - 1) // 2
    giver, receiver = tallies[1:1 + 2 * twos:2], tallies[2:2 + 2 * twos:2]
    margin = jnp.minimum(giver - 1, most - receiver)
    moved = jax.random.randint(jax.random.fold_in(key, 1), (twos,), 0, 1 << 20) % (margin + 1)
    tallies = tallies.at[1:1 + 2 * twos:2].set(giver - moved).at[2:2 + 2 * twos:2].set(receiver + moved)
    return tallies[jax.random.permutation(jax.random.fold_in(key, 2), amount)]


def scatter_about(own_key, shape, scale, most, cuts=(), held_as=jnp.bfloat16):
    gain = block_levels(own_key, shape, cuts, -0.22, 0.18) if cuts else 1.0
    entries = jax.random.normal(own_key, shape, jnp.float32) * scale * gain
    return jnp.minimum(jnp.maximum(entries, -most), most).astype(held_as)


def setup_inputs(seed: int = 0, part: int = 0) -> dict:
    arg_keys = jax.random.split(jax.random.key(seed), 7)
    part_splits = jax.random.split(jax.random.fold_in(arg_keys[6], part), 7)
    queries = draw_queries(jax.random.fold_in(jax.random.fold_in(arg_keys[6], part), 71), part)
    keys = draw_keys(jax.random.fold_in(jax.random.fold_in(arg_keys[6], part), 71), part)
    values = scatter_about(part_splits[2], (WINDOW_TOKENS, KEY_VALUE_HEADS * HEAD_DIMENSION), 1.0, 6.0, ((0, 32),))
    output_gradient = scatter_about(part_splits[3], (WINDOW_TOKENS, QUERY_HEADS * HEAD_DIMENSION), 1.0, 6.0, ((0, 32),))
    doc_lengths = ragged(part_splits[4], NDOCS, WINDOW_TOKENS, MOST, 2).astype(jnp.int32)
    span_order = jax.random.permutation(part_splits[5], NCHUNK).astype(jnp.int32)
    return {"queries": queries, "keys": keys, "values": values, "output_gradient": output_gradient, "doc_lengths": doc_lengths, "span_order": span_order}


def document_ids(doc_lengths, count):
    doc_ends = jnp.cumsum(doc_lengths).astype(jnp.int32)
    places = jnp.arange(count, dtype=jnp.int32)
    return jnp.sum((places[:, None] >= doc_ends[None, :]).astype(jnp.int32), axis=1).astype(jnp.int32)


def to_position(token_row_count, span_order):
    pieces = span_order.shape[0]
    blocks = token_row_count.reshape(pieces, token_row_count.shape[0] // pieces, token_row_count.shape[1])
    inverse = jnp.zeros((pieces,), jnp.int32).at[span_order].set(jnp.arange(pieces, dtype=jnp.int32))
    return blocks[inverse].reshape(token_row_count.shape)


def to_storage(token_row_count, span_order):
    pieces = span_order.shape[0]
    blocks = token_row_count.reshape(pieces, token_row_count.shape[0] // pieces, token_row_count.shape[1])
    return blocks[span_order].reshape(token_row_count.shape)


def padded(token_row_count, reach, fill):
    front = jnp.full((reach,) + token_row_count.shape[1:], fill, token_row_count.dtype)
    return jnp.concatenate([front, token_row_count], axis=0)


def window_probs(query_rows, key_window, docs, doc_pad, start, block, reach):
    width = query_rows.shape[1]
    query_docs = lax.dynamic_slice_in_dim(docs, start, block)
    key_docs = lax.dynamic_slice_in_dim(doc_pad, start, block + reach)
    query_place = start + jnp.arange(block, dtype=jnp.int32)
    key_place = start - reach + jnp.arange(block + reach, dtype=jnp.int32)
    visible = (key_docs[None, :] == query_docs[:, None]) & (key_place[None, :] <= query_place[:, None])
    scores = jnp.dot(query_rows, key_window.T, preferred_element_type=jnp.float32) * (width ** -0.5)
    scores = jnp.where(visible, scores, -jnp.inf)
    peak = jnp.max(scores, axis=1, keepdims=True)
    weights = jnp.exp(scores - peak)
    return weights / jnp.sum(weights, axis=1, keepdims=True)


def head_forward(query, keys, values, docs, block, reach):
    total_count = query.shape[0]
    key_pad = padded(keys, reach, 0)
    value_pad = padded(values, reach, 0)
    doc_pad = padded(docs, reach, -1)

    def one_block(block_index, result):
        start = (block_index * block).astype(jnp.int32)
        query_rows = lax.dynamic_slice_in_dim(query, start, block)
        key_window = lax.dynamic_slice_in_dim(key_pad, start, block + reach)
        value_window = lax.dynamic_slice_in_dim(value_pad, start, block + reach)
        probs = window_probs(query_rows, key_window, docs, doc_pad, start, block, reach).astype(jnp.bfloat16)
        mixed_layout = jnp.dot(probs, value_window, preferred_element_type=jnp.float32).astype(jnp.bfloat16)
        return lax.dynamic_update_slice_in_dim(result, mixed_layout, start, 0)

    return lax.fori_loop(0, total_count // block, one_block, jnp.zeros(query.shape, jnp.bfloat16))


def head_backward(query, keys, values, grad_out, docs, block, reach):
    total_count, width = query.shape
    key_pad = padded(keys, reach, 0)
    value_pad = padded(values, reach, 0)
    doc_pad = padded(docs, reach, -1)

    def one_block(block_index, carry):
        query_gradient, key_gradient, value_gradient = carry
        start = (block_index * block).astype(jnp.int32)
        query_rows = lax.dynamic_slice_in_dim(query, start, block)
        grad_rows = lax.dynamic_slice_in_dim(grad_out, start, block)
        key_window = lax.dynamic_slice_in_dim(key_pad, start, block + reach)
        value_window = lax.dynamic_slice_in_dim(value_pad, start, block + reach)
        probs = window_probs(query_rows, key_window, docs, doc_pad, start, block, reach)
        probs_low = probs.astype(jnp.bfloat16)
        grad_probs = jnp.dot(grad_rows, value_window.T, preferred_element_type=jnp.float32)
        centre = jnp.sum(probs * grad_probs, axis=1, keepdims=True)
        grad_scores = (probs * (grad_probs - centre) * (width ** -0.5)).astype(jnp.bfloat16)
        query_part = jnp.dot(grad_scores, key_window, preferred_element_type=jnp.float32).astype(jnp.bfloat16)
        key_part = jnp.dot(grad_scores.T, query_rows, preferred_element_type=jnp.float32)
        value_part = jnp.dot(probs_low.T, grad_rows, preferred_element_type=jnp.float32)
        query_gradient = lax.dynamic_update_slice_in_dim(query_gradient, query_part, start, 0)
        old_k = lax.dynamic_slice_in_dim(key_gradient, start, block + reach)
        old_v = lax.dynamic_slice_in_dim(value_gradient, start, block + reach)
        key_gradient = lax.dynamic_update_slice_in_dim(key_gradient, old_k + key_part, start, 0)
        value_gradient = lax.dynamic_update_slice_in_dim(value_gradient, old_v + value_part, start, 0)
        return query_gradient, key_gradient, value_gradient

    start_carry = (jnp.zeros(query.shape, jnp.bfloat16),
                   jnp.zeros((total_count + reach, width), jnp.float32),
                   jnp.zeros((total_count + reach, width), jnp.float32))
    query_gradient, key_gradient, value_gradient = lax.fori_loop(0, total_count // block, one_block, start_carry)
    return query_gradient, key_gradient[reach:], value_gradient[reach:]


def reference(queries, keys, values, output_gradient, doc_lengths, span_order):
    total_count = queries.shape[0]
    docs = document_ids(doc_lengths, total_count)
    head_group = QUERY_HEADS // KEY_VALUE_HEADS

    def head_major_layout(token_row_count, count):
        return to_position(token_row_count, span_order).reshape(total_count, count, HEAD_DIMENSION).transpose(1, 0, 2)

    query_head_rows = head_major_layout(queries, QUERY_HEADS).reshape(KEY_VALUE_HEADS, head_group, total_count, HEAD_DIMENSION)
    head_gradients = head_major_layout(output_gradient, QUERY_HEADS).reshape(KEY_VALUE_HEADS, head_group, total_count, HEAD_DIMENSION)
    key_head_rows = head_major_layout(keys, KEY_VALUE_HEADS)
    value_head_rows = head_major_layout(values, KEY_VALUE_HEADS)

    def per_group(inputs):
        query_group, key_head, value_head, grad_group = inputs

        def per_head(pair):
            query_head, grad_head = pair
            mixed_layout = head_forward(query_head, key_head, value_head, docs, QB, MOST)
            query_gradient, key_gradient, value_gradient = head_backward(query_head, key_head, value_head, grad_head, docs, QB, MOST)
            return mixed_layout, query_gradient, key_gradient, value_gradient

        mixed_layout, query_gradient, key_gradient, value_gradient = lax.map(per_head, (query_group, grad_group))
        return mixed_layout, query_gradient, jnp.sum(key_gradient, axis=0).astype(jnp.bfloat16), jnp.sum(value_gradient, axis=0).astype(jnp.bfloat16)

    mixed_layout, query_gradient, key_gradient, value_gradient = lax.map(per_group, (query_head_rows, key_head_rows, value_head_rows, head_gradients))

    def row_major_layout(heads, count):
        flat = heads.reshape(count, total_count, HEAD_DIMENSION).transpose(1, 0, 2).reshape(total_count, count * HEAD_DIMENSION)
        return to_storage(flat, span_order)

    return row_major_layout(mixed_layout, QUERY_HEADS), row_major_layout(query_gradient, QUERY_HEADS), row_major_layout(key_gradient, KEY_VALUE_HEADS), row_major_layout(value_gradient, KEY_VALUE_HEADS)
```

```python
import functools

import jax
import jax.numpy as jnp
from jax import lax
from jax.experimental import pallas as pl
from jax.experimental.pallas import tpu as pltpu
from jax.sharding import PartitionSpec as P

HD = 128
QH = 32
KH = 4
GH = QH // KH
C = 64
NB = 7
W = NB * C
NX = 4
GW = GH * HD
LOG2E = 1.4426950408889634
MESH = pl.DeviceIdType.MESH
F32 = jnp.float32
BF16 = jnp.bfloat16


def kernel(
    nz,
    q_ref,
    k_ref,
    v_ref,
    g_ref,
    len_ref,
    span_ref,
    inv_ref,
    o_out,
    gq_out,
    gk_out,
    gv_out,
    kv,
    qx,
    dx,
    ox,
    gx,
    ck,
    cv,
    send_buf,
    recv_buf,
    fin,
    loc_sem,
    xin_send,
    xin_recv,
    zin_send,
    zin_recv,
    xout_send,
    xout_recv,
    zout_send,
    zout_recv,
):
    half = nz // 2
    rows = q_ref.shape[0]
    per = rows // C
    me = lax.axis_index("ctx")
    x = me // nz
    z = lax.rem(me, nz)
    ndoc = len_ref.shape[0]

    def at_x(r):
        return lax.rem(x + r + NX, NX)

    def at_z(r):
        return lax.rem(z + r + nz, nz)

    def dev(xx, zz):
        return {"ctx": xx * nz + zz}

    def cols(g, width):
        return pl.ds(pl.multiple_of(g * width, width), width)

    def pblocks(piece):
        return pl.ds(piece * per, per)

    def prows(piece):
        return pl.ds(pl.multiple_of(piece * rows, rows), rows)

    own = z * NX + x
    local = [
        pltpu.make_async_copy(k_ref.at[:, :, cols(x, HD)], kv.at[0, pblocks(own)], loc_sem.at[0]),
        pltpu.make_async_copy(v_ref.at[:, :, cols(x, HD)], kv.at[1, pblocks(own)], loc_sem.at[1]),
        pltpu.make_async_copy(q_ref.at[:, cols(x, GW)], qx.at[prows(x)], loc_sem.at[2]),
        pltpu.make_async_copy(g_ref.at[:, cols(x, GW)], dx.at[prows(x)], loc_sem.at[3]),
    ]
    for c in local:
        c.start()

    barrier = pltpu.get_barrier_semaphore()
    peers = [dev(at_x(r), z) for r in (1, 2, 3)] + [dev(x, at_z(r)) for r in (1, -1)]
    for p in peers:
        pl.semaphore_signal(barrier, inc=1, device_id=p, device_id_type=MESH)
    pl.semaphore_wait(barrier, len(peers))

    def x_in(a, r):
        g = at_x(r)
        if a < 2:
            src, dst = (k_ref, v_ref)[a].at[:, :, cols(g, HD)], kv.at[a, pblocks(own)]
        else:
            src, dst = (q_ref, g_ref)[a - 2].at[:, cols(g, GW)], (qx, dx)[a - 2].at[prows(x)]
        return pltpu.make_async_remote_copy(
            src_ref=src,
            dst_ref=dst,
            send_sem=xin_send.at[a, r - 1],
            recv_sem=xin_recv.at[a, r - 1],
            device_id=dev(g, z),
            device_id_type=MESH,
        )

    def x_in_wait(a, r):
        src = at_x(-r)
        if a < 2:
            dst = kv.at[a, pblocks(z * NX + src)]
        else:
            dst = (qx, dx)[a - 2].at[prows(src)]
        pltpu.make_async_remote_copy(
            src_ref=dst,
            dst_ref=dst,
            send_sem=xin_send.at[a, r - 1],
            recv_sem=xin_recv.at[a, r - 1],
            device_id=dev(x, z),
            device_id_type=MESH,
        ).wait_recv()

    def z_in(d, h, s):
        sign = 1 - 2 * d
        piece = at_z(-sign * (h - 1)) * NX + s
        ref = kv.at[:, pblocks(piece)] if h < half else kv.at[d, pblocks(piece)]
        return pltpu.make_async_remote_copy(
            src_ref=ref,
            dst_ref=ref,
            send_sem=zin_send.at[d, h - 1, s],
            recv_sem=zin_recv.at[d, h - 1, s],
            device_id=dev(x, at_z(sign)),
            device_id_type=MESH,
        )

    def z_in_wait(d, h, s):
        sign = 1 - 2 * d
        piece = at_z(-sign * h) * NX + s
        ref = kv.at[:, pblocks(piece)] if h < half else kv.at[d, pblocks(piece)]
        pltpu.make_async_remote_copy(
            src_ref=ref,
            dst_ref=ref,
            send_sem=zin_send.at[d, h - 1, s],
            recv_sem=zin_recv.at[d, h - 1, s],
            device_id=dev(x, z),
            device_id_type=MESH,
        ).wait_recv()

    for r in (1, 3, 2):
        for a in (0, 1):
            x_in(a, r).start()
    local[0].wait()
    local[1].wait()
    for d in (0, 1):
        z_in(d, 1, x).start()
    for a in (2, 3):
        for r in (2, 1, 3):
            x_in(a, r).start()
    order = (1, 3, 2)
    for r in order:
        for a in (0, 1):
            x_in_wait(a, r)
        for d in (0, 1):
            z_in(d, 1, at_x(-r)).start()
    for h in range(1, half + 1):
        for r in (0,) + order:
            for d in (0, 1):
                z_in_wait(d, h, at_x(-r))
                if h < half:
                    z_in(d, h + 1, at_x(-r)).start()

    ends = []
    total = 0
    for n in range(ndoc):
        total = total + len_ref[n]
        ends.append(total)

    zero = jnp.zeros((C, HD), F32)
    for i in range(NX * per):
        for end in (0, NB + 1):
            ck[i, end] = zero
            cv[i, end] = zero

    local[2].wait()
    local[3].wait()
    for a in (2, 3):
        for r in (2, 1, 3):
            x_in_wait(a, r)

    def place(i):
        s, b = i // per, lax.rem(i, per)
        return span_ref[(s * nz + z) * per + b]

    def x_out(a, r):
        t = at_x(r)
        if a < 2:
            src, dst = (ox, gx)[a].at[prows(t)], (o_out, gq_out)[a].at[:, cols(x, GW)]
        else:
            src, dst = fin.at[a - 2, prows(t)], (gk_out, gv_out)[a - 2].at[:, cols(x, HD)]
        return pltpu.make_async_remote_copy(
            src_ref=src,
            dst_ref=dst,
            send_sem=xout_send.at[a, r - 1],
            recv_sem=xout_recv.at[a, r - 1],
            device_id=dev(t, z),
            device_id_type=MESH,
        )

    def x_out_wait(a, r):
        src = at_x(-r)
        if a < 2:
            dst = (o_out, gq_out)[a].at[:, cols(src, GW)]
        else:
            dst = (gk_out, gv_out)[a - 2].at[:, cols(src, HD)]
        pltpu.make_async_remote_copy(
            src_ref=dst,
            dst_ref=dst,
            send_sem=xout_send.at[a, r - 1],
            recv_sem=xout_recv.at[a, r - 1],
            device_id=dev(x, z),
            device_id_type=MESH,
        ).wait_recv()

    def local_out(a):
        if a < 2:
            src, dst = (ox, gx)[a].at[prows(x)], (o_out, gq_out)[a].at[:, cols(x, GW)]
        else:
            src, dst = fin.at[a - 2, prows(x)], (gk_out, gv_out)[a - 2].at[:, cols(x, HD)]
        return pltpu.make_async_copy(src, dst, loc_sem.at[4 + a])

    scale = HD**-0.5
    lane = lax.broadcasted_iota(jnp.int32, (1, HD), 1)
    row = lax.broadcasted_iota(jnp.int32, (W, HD), 0)

    def block(n, _):
        r = (2, 1, 3, 0)
        rel = jnp.where(n < per, r[0], jnp.where(n < 2 * per, r[1], jnp.where(n < 3 * per, r[2], r[3])))
        i = at_x(rel) * per + lax.rem(n, per)
        at = place(i)
        keys, vals = [], []
        for o in range(NB):
            e = inv_ref[jnp.maximum(at - (NB - 1) + o, 0)]
            keys.append(kv[0, e])
            vals.append(kv[1, e])
        key = jnp.concatenate(keys, axis=0)
        val = jnp.concatenate(vals, axis=0)
        mine = pl.ds(pl.multiple_of(i * C, C), C)
        query = jnp.concatenate([qx[mine, h * HD : (h + 1) * HD] for h in range(GH)], axis=0)
        grad = jnp.concatenate([dx[mine, h * HD : (h + 1) * HD] for h in range(GH)], axis=0)
        pos = at * C + lax.rem(lane, C)
        first = jnp.zeros_like(pos)
        for end in ends:
            first = jnp.where(pos >= end, end, first)
        t = row + (at - (NB - 1)) * C
        seen = jnp.logical_and(t >= first, t <= pos)
        seen = jnp.concatenate([seen] * (GH * C // HD), axis=1)

        def nt(a, b):
            return lax.dot_general(a, b, (((1,), (1,)), ((), ())), preferred_element_type=F32)

        def tn(a, b):
            return lax.dot_general(a, b, (((0,), (0,)), ((), ())), preferred_element_type=F32)

        scores = jnp.where(seen, nt(key, query), -jnp.inf)
        peak = jnp.max(scores, axis=0, keepdims=True)
        weights = jnp.exp2((scores - peak) * (scale * LOG2E))
        probs = weights * (1.0 / jnp.sum(weights, axis=0, keepdims=True))
        low = probs.astype(BF16)
        mixed = tn(val, low).T.astype(BF16)
        grad_probs = nt(val, grad)
        centre = jnp.sum(probs * grad_probs, axis=0, keepdims=True)
        grad_scores = (probs * (grad_probs - centre)).astype(BF16)
        query_grad = (tn(key, grad_scores) * scale).T.astype(BF16)
        for h in range(GH):
            ox[mine, h * HD : (h + 1) * HD] = mixed[h * C : (h + 1) * C]
            gx[mine, h * HD : (h + 1) * HD] = query_grad[h * C : (h + 1) * C]
        key_grad = jnp.dot(grad_scores, query, preferred_element_type=F32) * scale
        val_grad = jnp.dot(low, grad, preferred_element_type=F32)
        ck[i, pl.ds(1, NB)] = key_grad.reshape(NB, C, HD)
        cv[i, pl.ds(1, NB)] = val_grad.reshape(NB, C, HD)

        for m, r_out in enumerate(r[:3]):

            @pl.when(n == (m + 1) * per - 1)
            def _():
                for a in (0, 1):
                    x_out(a, r_out).start()

        return 0

    lax.fori_loop(0, NX * per, block, 0)
    for a in (0, 1):
        local_out(a).start()

    def part(zz, s, b, which):
        at = span_ref[(s * nz + zz) * per + b]
        out = []
        for w in which:
            out.append(jnp.zeros((C, HD), F32))
        for i in range(NX * per):
            o = jnp.minimum(jnp.maximum(at - place(i) + NB, 0), NB + 1)
            for n, w in enumerate(which):
                out[n] = out[n] + (ck, cv)[w][i, o]
        return out

    def z_out(d, h, s):
        sign = 1 - 2 * d
        if h == 1:
            src, dst = send_buf.at[d, h - 1, s, d], recv_buf.at[d, h - 1, s, d]
        else:
            src, dst = send_buf.at[d, h - 1, s], recv_buf.at[d, h - 1, s]
        return pltpu.make_async_remote_copy(
            src_ref=src,
            dst_ref=dst,
            send_sem=zout_send.at[d, h - 1, s],
            recv_sem=zout_recv.at[d, h - 1, s],
            device_id=dev(x, at_z(sign)),
            device_id_type=MESH,
        )

    for h in range(1, half + 1):

        def reduce_step(s, _):
            for d in (0, 1):
                sign = 1 - 2 * d
                owner = at_z(sign * (half + 1 - h))
                which = (d,) if h == 1 else (0, 1)
                if h > 1:
                    z_out(d, h - 1, s).wait_recv()
                for b in range(per):
                    there = pl.ds(b * C, C)
                    for w, sums in zip(which, part(owner, s, b, which)):
                        if h > 2 or (h == 2 and w == d):
                            sums = sums + recv_buf[d, h - 2, s, w, there].astype(F32)
                        send_buf[d, h - 1, s, w, there] = sums.astype(BF16)
                z_out(d, h, s).start()
            return 0

        lax.fori_loop(0, NX, reduce_step, 0)

    def last_step(n, _):
        s = at_x(n + 1)
        for d in (0, 1):
            z_out(d, half, s).wait_recv()
        for b in range(per):
            there = pl.ds(b * C, C)
            for w, sums in enumerate(part(z, s, b, (0, 1))):
                for d in (0, 1):
                    sums = sums + recv_buf[d, half - 1, s, w, there].astype(F32)
                fin[w, pl.ds(pl.multiple_of(s * rows + b * C, C), C)] = sums.astype(BF16)
        for r in (1, 2, 3):

            @pl.when(n == r - 1)
            def _():
                for a in (2, 3):
                    x_out(a, r).start()

        return 0

    lax.fori_loop(0, NX, last_step, 0)
    for a in (2, 3):
        local_out(a).start()

    for a in range(4):
        local_out(a).wait()
        for r in (1, 2, 3):
            x_out_wait(a, r)
            x_out(a, r).wait_send()
            x_in(a, r).wait_send()
    for d in (0, 1):
        for h in range(1, half + 1):
            for s in range(NX):
                z_in(d, h, s).wait_send()
                z_out(d, h, s).wait_send()


def local(queries, keys, values, output_gradient, doc_lengths, span_order):
    nz = lax.axis_size("ctx") // NX
    half = nz // 2
    rows = queries.shape[0]
    per = rows // C
    tokens = rows * NX * nz
    blocks = tokens // C
    places = jnp.arange(blocks, dtype=jnp.int32)
    owner = places // per
    slot = ((owner % nz) * NX + owner // nz) * per + places % per
    inverse = jnp.sum(
        jnp.where(span_order[None, :] == places[:, None], slot[None, :], 0), axis=1, dtype=jnp.int32
    )
    hbm = pl.BlockSpec(memory_space=pl.ANY)
    smem = pl.BlockSpec(memory_space=pltpu.SMEM)
    dma = pltpu.SemaphoreType.DMA
    return pl.pallas_call(
        functools.partial(kernel, nz),
        out_shape=(
            jax.ShapeDtypeStruct(queries.shape, BF16),
            jax.ShapeDtypeStruct(queries.shape, BF16),
            jax.ShapeDtypeStruct(keys.shape, BF16),
            jax.ShapeDtypeStruct(keys.shape, BF16),
        ),
        in_specs=[hbm] * 4 + [smem] * 3,
        out_specs=(hbm,) * 4,
        scratch_shapes=[
            pltpu.VMEM((2, blocks, C, HD), BF16),
            pltpu.VMEM((NX * rows, GW), BF16),
            pltpu.VMEM((NX * rows, GW), BF16),
            pltpu.VMEM((NX * rows, GW), BF16),
            pltpu.VMEM((NX * rows, GW), BF16),
            pltpu.VMEM((NX * per, NB + 2, C, HD), F32),
            pltpu.VMEM((NX * per, NB + 2, C, HD), F32),
            pltpu.VMEM((2, half, NX, 2, rows, HD), BF16),
            pltpu.VMEM((2, half, NX, 2, rows, HD), BF16),
            pltpu.VMEM((2, NX * rows, HD), BF16),
            dma((8,)),
            dma((4, 3)),
            dma((4, 3)),
            dma((2, half, NX)),
            dma((2, half, NX)),
            dma((4, 3)),
            dma((4, 3)),
            dma((2, half, NX)),
            dma((2, half, NX)),
        ],
        compiler_params=pltpu.CompilerParams(
            collective_id=0, has_side_effects=True, vmem_limit_bytes=56 * 2**20
        ),
    )(queries, keys.reshape(per, C, KH * HD), values.reshape(per, C, KH * HD), output_gradient, doc_lengths, span_order, inverse)


def solution(mesh):
    wide = P(("dp", "ctx"), None)
    return jax.shard_map(
        local,
        mesh=mesh,
        in_specs=(wide, wide, wide, wide, P("dp"), P("dp")),
        out_specs=(wide, wide, wide, wide),
        check_vma=False,
    )
```

```python
import functools

import jax
import jax.numpy as jnp
from jax import lax
from jax.experimental import pallas as pl
from jax.experimental.pallas import tpu as pltpu
from jax.sharding import PartitionSpec as P

HD = 128
QH = 32
KH = 4
GH = QH // KH
C = 64
NB = 7
W = NB * C
NX = 4
GW = GH * HD
LOG2E = 1.4426950408889634
MESH = pl.DeviceIdType.MESH
F32 = jnp.float32
BF16 = jnp.bfloat16


def kernel(
    nz,
    q_ref,
    k_ref,
    v_ref,
    g_ref,
    len_ref,
    span_ref,
    o_out,
    gq_out,
    gk_out,
    gv_out,
    keys,
    vals,
    qx,
    dx,
    ox,
    gx,
    pb,
    ck,
    cv,
    send_buf,
    recv_buf,
    fin,
    inv_row,
    inv_ref,
    loc_sem,
    xin_send,
    xin_recv,
    zin_send,
    zin_recv,
    xout_send,
    xout_recv,
    zout_send,
    zout_recv,
):
    half = nz // 2
    rows = q_ref.shape[0]
    per = rows // C
    kv = (keys, vals)
    blocks = keys.shape[0]
    me = lax.axis_index("ctx")
    x = me // nz
    z = lax.rem(me, nz)

    def at_x(r):
        return lax.rem(x + r + NX, NX)

    def at_z(r):
        return lax.rem(z + r + nz, nz)

    def dev(xx, zz):
        return {"ctx": xx * nz + zz}

    def cols(g, width):
        return pl.ds(pl.multiple_of(g * width, width), width)

    def pblocks(piece):
        return pl.ds(piece * per, per)

    def prows(piece):
        return pl.ds(pl.multiple_of(piece * rows, rows), rows)

    own = z * NX + x
    local = [
        pltpu.make_async_copy(k_ref.at[:, :, cols(x, HD)], keys.at[pblocks(own)], loc_sem.at[0]),
        pltpu.make_async_copy(v_ref.at[:, :, cols(x, HD)], vals.at[pblocks(own)], loc_sem.at[1]),
        pltpu.make_async_copy(q_ref.at[:, cols(x, GW)], qx.at[prows(x)], loc_sem.at[2]),
        pltpu.make_async_copy(g_ref.at[:, cols(x, GW)], dx.at[prows(x)], loc_sem.at[3]),
    ]
    for c in local:
        c.start()

    barrier = pltpu.get_barrier_semaphore()
    peers = [dev(at_x(r), z) for r in (1, 2, 3)] + [dev(x, at_z(r)) for r in (1, -1)]
    for p in peers:
        pl.semaphore_signal(barrier, inc=1, device_id=p, device_id_type=MESH)
    pl.semaphore_wait(barrier, len(peers))

    def x_in(a, r):
        g = at_x(r)
        if a < 2:
            src, dst = (k_ref, v_ref)[a].at[:, :, cols(g, HD)], kv[a].at[pblocks(own)]
        else:
            src, dst = (q_ref, g_ref)[a - 2].at[:, cols(g, GW)], (qx, dx)[a - 2].at[prows(x)]
        return pltpu.make_async_remote_copy(
            src_ref=src,
            dst_ref=dst,
            send_sem=xin_send.at[a, r - 1],
            recv_sem=xin_recv.at[a, r - 1],
            device_id=dev(g, z),
            device_id_type=MESH,
        )

    def x_in_wait(a, r):
        src = at_x(-r)
        if a < 2:
            dst = kv[a].at[pblocks(z * NX + src)]
        else:
            dst = (qx, dx)[a - 2].at[prows(src)]
        pltpu.make_async_remote_copy(
            src_ref=dst,
            dst_ref=dst,
            send_sem=xin_send.at[a, r - 1],
            recv_sem=xin_recv.at[a, r - 1],
            device_id=dev(x, z),
            device_id_type=MESH,
        ).wait_recv()

    def z_in_ref(w, d, h, piece):
        if h < half:
            return kv[w].at[pblocks(piece)]
        return kv[w].at[pl.ds(piece * per + d, 1)]

    def z_in(w, d, h, s):
        sign = 1 - 2 * d
        ref = z_in_ref(w, d, h, at_z(-sign * (h - 1)) * NX + s)
        return pltpu.make_async_remote_copy(
            src_ref=ref,
            dst_ref=ref,
            send_sem=zin_send.at[w, d, h - 1, s],
            recv_sem=zin_recv.at[w, d, h - 1, s],
            device_id=dev(x, at_z(sign)),
            device_id_type=MESH,
        )

    def z_in_wait(w, d, h, s):
        sign = 1 - 2 * d
        ref = z_in_ref(w, d, h, at_z(-sign * h) * NX + s)
        pltpu.make_async_remote_copy(
            src_ref=ref,
            dst_ref=ref,
            send_sem=zin_send.at[w, d, h - 1, s],
            recv_sem=zin_recv.at[w, d, h - 1, s],
            device_id=dev(x, z),
            device_id_type=MESH,
        ).wait_recv()

    order = (0, 1, 3, 2)

    def z_in_pass(w, h, k):
        s = at_x(-order[k])
        for d in (0, 1):
            z_in_wait(w, d, h, s)
            if h < half:
                z_in(w, d, h + 1, s).start()

    def z_in_first(w, k):
        if k > 0:
            x_in_wait(w, order[k])
        for d in (0, 1):
            z_in(w, d, 1, at_x(-order[k])).start()

    for r in (1, 3, 2):
        x_in(0, r).start()
    local[0].wait()
    z_in_first(0, 0)
    for r in (1, 3, 2):
        x_in(1, r).start()
    for a in (2, 3):
        for r in (1, 3):
            x_in(a, r).start()

    at_lane = lax.broadcasted_iota(jnp.int32, inv_row.shape, 1)
    inverse = jnp.zeros(inv_row.shape, jnp.int32)
    for j in range(blocks):
        owner = j // per
        inverse = jnp.where(
            at_lane == span_ref[j], ((owner % nz) * NX + owner // nz) * per + j % per, inverse
        )
    inv_row[...] = inverse
    look = pltpu.make_async_copy(inv_row, inv_ref, loc_sem.at[8])
    look.start()

    for k in (1, 2, 3):
        z_in_first(0, k)
    for h in range(1, half):
        for k in range(NX):
            z_in_pass(0, h, k)

    ends = []
    total = 0
    for n in range(len_ref.shape[0]):
        total = total + len_ref[n]
        ends.append(total)

    zero = jnp.zeros((C, HD), F32)
    for i in range(NX * per):
        for end in (0, NB + 1):
            ck[i, end] = zero
            cv[i, end] = zero

    local[1].wait()
    for k in range(NX):
        z_in_first(1, k)
    for k in range(NX):
        z_in_pass(0, half, k)
    look.wait()
    local[2].wait()
    local[3].wait()

    def place(i):
        s, b = i // per, lax.rem(i, per)
        return span_ref[(s * nz + z) * per + b]

    def x_out(a, r):
        t = at_x(r)
        if a < 2:
            src, dst = (ox, gx)[a].at[prows(t)], (o_out, gq_out)[a].at[:, cols(x, GW)]
        else:
            src, dst = fin.at[a - 2, prows(t)], (gk_out, gv_out)[a - 2].at[:, cols(x, HD)]
        return pltpu.make_async_remote_copy(
            src_ref=src,
            dst_ref=dst,
            send_sem=xout_send.at[a, r - 1],
            recv_sem=xout_recv.at[a, r - 1],
            device_id=dev(t, z),
            device_id_type=MESH,
        )

    def x_out_wait(a, r):
        src = at_x(-r)
        if a < 2:
            dst = (o_out, gq_out)[a].at[:, cols(src, GW)]
        else:
            dst = (gk_out, gv_out)[a - 2].at[:, cols(src, HD)]
        pltpu.make_async_remote_copy(
            src_ref=dst,
            dst_ref=dst,
            send_sem=xout_send.at[a, r - 1],
            recv_sem=xout_recv.at[a, r - 1],
            device_id=dev(x, z),
            device_id_type=MESH,
        ).wait_recv()

    def local_out(a):
        if a < 2:
            src, dst = (ox, gx)[a].at[prows(x)], (o_out, gq_out)[a].at[:, cols(x, GW)]
        else:
            src, dst = fin.at[a - 2, prows(x)], (gk_out, gv_out)[a - 2].at[:, cols(x, HD)]
        return pltpu.make_async_copy(src, dst, loc_sem.at[4 + a])

    def part(w, zz, s, b):
        at = span_ref[(s * nz + zz) * per + b]
        out = None
        for i in range(NX * per):
            o = jnp.minimum(jnp.maximum(at - place(i) + NB, 0), NB + 1)
            term = (ck, cv)[w][i, o]
            out = term if out is None else out + term
        return out

    def z_out(w, d, h, s):
        sign = 1 - 2 * d
        there = (w, d, h - 1, s, d) if h == 1 else (w, d, h - 1, s)
        return pltpu.make_async_remote_copy(
            src_ref=send_buf.at[there],
            dst_ref=recv_buf.at[there],
            send_sem=zout_send.at[w, d, h - 1, s],
            recv_sem=zout_recv.at[w, d, h - 1, s],
            device_id=dev(x, at_z(sign)),
            device_id_type=MESH,
        )

    def pick(n, rels):
        rel = rels[-1]
        for m in range(len(rels) - 2, -1, -1):
            rel = jnp.where(n <= m, rels[m], rel)
        return rel

    def z_out_hop(w, h):
        def step(n, _):
            s = at_x(pick(n, (2, 1, 3, 0)))
            for d in (0, 1):
                sign = 1 - 2 * d
                owner = at_z(sign * (half + 1 - h))
                if h > 1:
                    z_out(w, d, h - 1, s).wait_recv()
                for b in range(per):
                    if h == 1 and b != d:
                        continue
                    sums = part(w, owner, s, b)
                    if h > 2 or (h == 2 and b == d):
                        sums = sums + recv_buf[w, d, h - 2, s, b].astype(F32)
                    send_buf[w, d, h - 1, s, b] = sums.astype(BF16)
                z_out(w, d, h, s).start()
            return 0

        lax.fori_loop(0, NX, step, 0)

    def z_out_last(w):
        def step(n, _):
            s = at_x(pick(n, (2, 1, 3, 0)))
            for d in (0, 1):
                z_out(w, d, half, s).wait_recv()
            for b in range(per):
                sums = part(w, z, s, b)
                for d in (0, 1):
                    sums = sums + recv_buf[w, d, half - 1, s, b].astype(F32)
                fin[w, pl.ds(pl.multiple_of(s * rows + b * C, C), C)] = sums.astype(BF16)
            for m, r in enumerate((2, 1, 3)):

                @pl.when(n == m)
                def _():
                    x_out(2 + w, r).start()

            return 0

        lax.fori_loop(0, NX, step, 0)
        local_out(2 + w).start()

    scale = HD**-0.5
    lane = lax.broadcasted_iota(jnp.int32, (1, HD), 1)
    row = lax.broadcasted_iota(jnp.int32, (W, HD), 0)

    def nt(a, b):
        return lax.dot_general(a, b, (((1,), (1,)), ((), ())), preferred_element_type=F32)

    def tn(a, b):
        return lax.dot_general(a, b, (((0,), (0,)), ((), ())), preferred_element_type=F32)

    def window(w, at):
        found = [kv[w][inv_ref[0, jnp.maximum(at - (NB - 1) + o, 0)]] for o in range(NB)]
        return jnp.concatenate(found, axis=0)

    def stacked(ref, mine):
        return jnp.concatenate([ref[mine, h * HD : (h + 1) * HD] for h in range(GH)], axis=0)

    def unstack(ref, mine, value):
        for h in range(GH):
            ref[mine, h * HD : (h + 1) * HD] = value[h * C : (h + 1) * C]

    def first_half(i):
        at = place(i)
        mine = pl.ds(pl.multiple_of(i * C, C), C)
        pos = at * C + lax.rem(lane, C)
        first = jnp.zeros_like(pos)
        for end in ends:
            first = jnp.where(pos >= end, end, first)
        t = row + (at - (NB - 1)) * C
        seen = jnp.logical_and(t >= first, t <= pos)
        seen = jnp.concatenate([seen] * (GH * C // HD), axis=1)
        scores = jnp.where(seen, nt(window(0, at), stacked(qx, mine)), -jnp.inf)
        peak = jnp.max(scores, axis=0, keepdims=True)
        weights = jnp.exp2((scores - peak) * (scale * LOG2E))
        probs = weights * (1.0 / jnp.sum(weights, axis=0, keepdims=True))
        pb[i] = probs
        val_grad = jnp.dot(probs.astype(BF16), stacked(dx, mine), preferred_element_type=F32)
        cv[i, pl.ds(1, NB)] = val_grad.reshape(NB, C, HD)

    def second_half(i):
        at = place(i)
        mine = pl.ds(pl.multiple_of(i * C, C), C)
        key, val = window(0, at), window(1, at)
        probs = pb[i]
        unstack(ox, mine, tn(val, probs.astype(BF16)).T.astype(BF16))
        grad_probs = nt(val, stacked(dx, mine))
        centre = jnp.sum(probs * grad_probs, axis=0, keepdims=True)
        grad_scores = (probs * (grad_probs - centre)).astype(BF16)
        unstack(gx, mine, (tn(key, grad_scores) * scale).T.astype(BF16))
        key_grad = jnp.dot(grad_scores, stacked(qx, mine), preferred_element_type=F32) * scale
        ck[i, pl.ds(1, NB)] = key_grad.reshape(NB, C, HD)

    near = 3 * per

    def passes(todo):
        for h, k in todo:
            z_in_pass(1, h, k)

    hops = [(h, k) for h in range(1, half + 1) for k in range(NX)]
    cuts = (0, 1, 5, 6, 7, 9, len(hops))

    def step(n, _):
        for m in range(1, near + 1):

            @pl.when(n == m)
            def _():
                passes(hops[cuts[m - 1] : cuts[m]])

        for m, r in ((per, 1), (2 * per, 3), (2 * near, 2)):

            @pl.when(n == m)
            def _():
                for a in (2, 3):
                    x_in_wait(a, r)
                if r != 2:
                    x_in(2 if r == 1 else 3, 2).start()

        @pl.when(n == 2 * near + per)
        def _():
            z_out_hop(1, 1)

        early = n < 2 * near
        stage = jnp.where(early, n // near, (n - 2 * near) // per)
        group = jnp.where(early, lax.rem(n, near) // per, 3)
        i = at_x(-pick(group, (0, 1, 3, 2))) * per + lax.rem(n, per)

        @pl.when(stage == 0)
        def _():
            first_half(i)

        @pl.when(stage == 1)
        def _():
            second_half(i)

        for m, r in ((near + 2 * per, 3), (near + 3 * per, 1), (2 * near + 2 * per, 2)):

            @pl.when(n == m - 1)
            def _():
                for a in (0, 1):
                    x_out(a, r).start()

        return 0

    lax.fori_loop(0, 2 * NX * per, step, 0)
    for a in (0, 1):
        local_out(a).start()
    for h in range(2, half + 1):
        z_out_hop(1, h)
    z_out_hop(0, 1)
    z_out_last(1)
    for h in range(2, half + 1):
        z_out_hop(0, h)
    z_out_last(0)

    for a in range(4):
        local_out(a).wait()
        for r in (1, 2, 3):
            x_out_wait(a, r)
            x_out(a, r).wait_send()
            x_in(a, r).wait_send()
    for w in (0, 1):
        for d in (0, 1):
            for h in range(1, half + 1):
                for s in range(NX):
                    z_in(w, d, h, s).wait_send()
                    z_out(w, d, h, s).wait_send()


def settle(*refs):
    srcs, dsts, sem = refs[:4], refs[4:8], refs[8]
    copies = []
    for n, (src, dst) in enumerate(zip(srcs, dsts)):
        parts = 4 if n < 2 else 1
        count = src.shape[0] // parts
        for m in range(parts):
            there = pl.ds(m * count, count)
            copies.append(pltpu.make_async_copy(src.at[there], dst.at[there], sem.at[n * 4 + m]))
    for c in copies:
        c.start()
    for c in copies:
        c.wait()


def local(queries, keys, values, output_gradient, doc_lengths, span_order):
    nz = lax.axis_size("ctx") // NX
    half = nz // 2
    rows = queries.shape[0]
    per = rows // C
    blocks = per * NX * nz
    hbm = pl.BlockSpec(memory_space=pl.ANY)
    smem = pl.BlockSpec(memory_space=pltpu.SMEM)
    dma = pltpu.SemaphoreType.DMA
    outs = (
        jax.ShapeDtypeStruct(queries.shape, BF16),
        jax.ShapeDtypeStruct(queries.shape, BF16),
        jax.ShapeDtypeStruct(keys.shape, BF16),
        jax.ShapeDtypeStruct(keys.shape, BF16),
    )
    results = pl.pallas_call(
        functools.partial(kernel, nz),
        out_shape=outs,
        in_specs=[hbm] * 4 + [smem] * 2,
        out_specs=(hbm,) * 4,
        scratch_shapes=[
            pltpu.VMEM((blocks, C, HD), BF16),
            pltpu.VMEM((blocks, C, HD), BF16),
            pltpu.VMEM((NX * rows, GW), BF16),
            pltpu.VMEM((NX * rows, GW), BF16),
            pltpu.VMEM((NX * rows, GW), BF16),
            pltpu.VMEM((NX * rows, GW), BF16),
            pltpu.VMEM((NX * per, W, GH * C), F32),
            pltpu.VMEM((NX * per, NB + 2, C, HD), F32),
            pltpu.VMEM((NX * per, NB + 2, C, HD), F32),
            pltpu.VMEM((2, 2, half, NX, per, C, HD), BF16),
            pltpu.VMEM((2, 2, half, NX, per, C, HD), BF16),
            pltpu.VMEM((2, NX * rows, HD), BF16),
            pltpu.VMEM((8, 128), jnp.int32),
            pltpu.SMEM((8, 128), jnp.int32),
            dma((9,)),
            dma((4, 3)),
            dma((4, 3)),
            dma((2, 2, half, NX)),
            dma((2, 2, half, NX)),
            dma((4, 3)),
            dma((4, 3)),
            dma((2, 2, half, NX)),
            dma((2, 2, half, NX)),
        ],
        compiler_params=pltpu.CompilerParams(
            collective_id=0, has_side_effects=True, vmem_limit_bytes=56 * 2**20
        ),
    )(
        queries,
        keys.reshape(per, C, KH * HD),
        values.reshape(per, C, KH * HD),
        output_gradient,
        doc_lengths,
        span_order,
    )
    return pl.pallas_call(
        settle,
        out_shape=outs,
        in_specs=[hbm] * 4,
        out_specs=(hbm,) * 4,
        scratch_shapes=[dma((16,))],
    )(*results)


def solution(mesh):
    wide = P(("dp", "ctx"), None)
    return jax.shard_map(
        local,
        mesh=mesh,
        in_specs=(wide, wide, wide, wide, P("dp"), P("dp")),
        out_specs=(wide, wide, wide, wide),
        check_vma=False,
    )
```

```python
import functools

import jax
import jax.numpy as jnp
from jax import lax
from jax.experimental import pallas as pl
from jax.experimental.pallas import tpu as pltpu
from jax.sharding import PartitionSpec as P

HD = 128
QH = 32
KH = 4
GH = QH // KH
C = 64
NB = 7
W = NB * C
NX = 4
GW = GH * HD
LOG2E = 1.4426950408889634
MESH = pl.DeviceIdType.MESH
F32 = jnp.float32
BF16 = jnp.bfloat16


def kernel(
    nz,
    q_ref,
    k_ref,
    v_ref,
    g_ref,
    len_ref,
    span_ref,
    o_out,
    gq_out,
    gk_out,
    gv_out,
    kv,
    qx,
    dx,
    ox,
    gx,
    ck,
    cv,
    send_buf,
    recv_buf,
    fin,
    inv_row,
    inv_ref,
    loc_sem,
    xin_send,
    xin_recv,
    zin_send,
    zin_recv,
    xout_send,
    xout_recv,
    zout_send,
    zout_recv,
):
    half = nz // 2
    rows = q_ref.shape[0]
    per = rows // C
    blocks = kv.shape[1]
    me = lax.axis_index("ctx")
    x = me // nz
    z = lax.rem(me, nz)

    def at_x(r):
        return lax.rem(x + r + NX, NX)

    def at_z(r):
        return lax.rem(z + r + nz, nz)

    def dev(xx, zz):
        return {"ctx": xx * nz + zz}

    def cols(g, width):
        return pl.ds(pl.multiple_of(g * width, width), width)

    def pblocks(piece):
        return pl.ds(piece * per, per)

    def prows(piece):
        return pl.ds(pl.multiple_of(piece * rows, rows), rows)

    own = z * NX + x
    local = [
        pltpu.make_async_copy(k_ref.at[:, :, cols(x, HD)], kv.at[0, pblocks(own)], loc_sem.at[0]),
        pltpu.make_async_copy(v_ref.at[:, :, cols(x, HD)], kv.at[1, pblocks(own)], loc_sem.at[1]),
        pltpu.make_async_copy(q_ref.at[:, cols(x, GW)], qx.at[prows(x)], loc_sem.at[2]),
        pltpu.make_async_copy(g_ref.at[:, cols(x, GW)], dx.at[prows(x)], loc_sem.at[3]),
    ]
    for c in local:
        c.start()

    barrier = pltpu.get_barrier_semaphore()
    peers = [dev(at_x(r), z) for r in (1, 2, 3)] + [dev(x, at_z(r)) for r in (1, -1)]
    for p in peers:
        pl.semaphore_signal(barrier, inc=1, device_id=p, device_id_type=MESH)
    pl.semaphore_wait(barrier, len(peers))

    def x_in(a, r):
        g = at_x(r)
        if a < 2:
            src, dst = (k_ref, v_ref)[a].at[:, :, cols(g, HD)], kv.at[a, pblocks(own)]
        else:
            src, dst = (q_ref, g_ref)[a - 2].at[:, cols(g, GW)], (qx, dx)[a - 2].at[prows(x)]
        return pltpu.make_async_remote_copy(
            src_ref=src,
            dst_ref=dst,
            send_sem=xin_send.at[a, r - 1],
            recv_sem=xin_recv.at[a, r - 1],
            device_id=dev(g, z),
            device_id_type=MESH,
        )

    def x_in_wait(a, r):
        src = at_x(-r)
        if a < 2:
            dst = kv.at[a, pblocks(z * NX + src)]
        else:
            dst = (qx, dx)[a - 2].at[prows(src)]
        pltpu.make_async_remote_copy(
            src_ref=dst,
            dst_ref=dst,
            send_sem=xin_send.at[a, r - 1],
            recv_sem=xin_recv.at[a, r - 1],
            device_id=dev(x, z),
            device_id_type=MESH,
        ).wait_recv()

    def z_in_ref(d, h, piece):
        return kv.at[:, pblocks(piece)] if h < half else kv.at[d, pblocks(piece)]

    def z_in(d, h, s):
        sign = 1 - 2 * d
        ref = z_in_ref(d, h, at_z(-sign * (h - 1)) * NX + s)
        return pltpu.make_async_remote_copy(
            src_ref=ref,
            dst_ref=ref,
            send_sem=zin_send.at[d, h - 1, s],
            recv_sem=zin_recv.at[d, h - 1, s],
            device_id=dev(x, at_z(sign)),
            device_id_type=MESH,
        )

    def z_in_wait(d, h, s):
        sign = 1 - 2 * d
        ref = z_in_ref(d, h, at_z(-sign * h) * NX + s)
        pltpu.make_async_remote_copy(
            src_ref=ref,
            dst_ref=ref,
            send_sem=zin_send.at[d, h - 1, s],
            recv_sem=zin_recv.at[d, h - 1, s],
            device_id=dev(x, z),
            device_id_type=MESH,
        ).wait_recv()

    order = (0, 1, 3, 2)

    for r in (1, 3, 2):
        for a in (0, 1):
            x_in(a, r).start()
    local[0].wait()
    local[1].wait()
    for d in (0, 1):
        z_in(d, 1, x).start()
    for r in order[1:]:
        for a in (2, 3):
            x_in(a, r).start()

    at_lane = lax.broadcasted_iota(jnp.int32, inv_row.shape, 1)
    inverse = jnp.zeros(inv_row.shape, jnp.int32)
    for j in range(blocks):
        owner = j // per
        inverse = jnp.where(
            at_lane == span_ref[j], ((owner % nz) * NX + owner // nz) * per + j % per, inverse
        )
    inv_row[...] = inverse
    look = pltpu.make_async_copy(inv_row, inv_ref, loc_sem.at[8])
    look.start()

    for r in order[1:]:
        for a in (0, 1):
            x_in_wait(a, r)
        for d in (0, 1):
            z_in(d, 1, at_x(-r)).start()
    ends = []
    total = 0
    for n in range(len_ref.shape[0]):
        total = total + len_ref[n]
        ends.append(total)

    zero = jnp.zeros((C, HD), F32)
    for i in range(NX * per):
        for end in (0, NB + 1):
            ck[i, end] = zero
            cv[i, end] = zero

    for h in range(1, half + 1):
        for r in order:
            for d in (0, 1):
                z_in_wait(d, h, at_x(-r))
                if h < half:
                    z_in(d, h + 1, at_x(-r)).start()
    look.wait()
    local[2].wait()
    local[3].wait()

    def place(i):
        s, b = i // per, lax.rem(i, per)
        return span_ref[(s * nz + z) * per + b]

    def x_out(a, r):
        t = at_x(r)
        if a < 2:
            src, dst = (ox, gx)[a].at[prows(t)], (o_out, gq_out)[a].at[:, cols(x, GW)]
        else:
            src, dst = fin.at[a - 2, prows(t)], (gk_out, gv_out)[a - 2].at[:, cols(x, HD)]
        return pltpu.make_async_remote_copy(
            src_ref=src,
            dst_ref=dst,
            send_sem=xout_send.at[a, r - 1],
            recv_sem=xout_recv.at[a, r - 1],
            device_id=dev(t, z),
            device_id_type=MESH,
        )

    def x_out_wait(a, r):
        src = at_x(-r)
        if a < 2:
            dst = (o_out, gq_out)[a].at[:, cols(src, GW)]
        else:
            dst = (gk_out, gv_out)[a - 2].at[:, cols(src, HD)]
        pltpu.make_async_remote_copy(
            src_ref=dst,
            dst_ref=dst,
            send_sem=xout_send.at[a, r - 1],
            recv_sem=xout_recv.at[a, r - 1],
            device_id=dev(x, z),
            device_id_type=MESH,
        ).wait_recv()

    def local_out(a):
        if a < 2:
            src, dst = (ox, gx)[a].at[prows(x)], (o_out, gq_out)[a].at[:, cols(x, GW)]
        else:
            src, dst = fin.at[a - 2, prows(x)], (gk_out, gv_out)[a - 2].at[:, cols(x, HD)]
        return pltpu.make_async_copy(src, dst, loc_sem.at[4 + a])

    def part(w, zz, s, b):
        at = span_ref[(s * nz + zz) * per + b]
        out = None
        for i in range(NX * per):
            o = jnp.minimum(jnp.maximum(at - place(i) + NB, 0), NB + 1)
            term = (ck, cv)[w][i, o]
            out = term if out is None else out + term
        return out

    def z_out(d, h, s):
        sign = 1 - 2 * d
        there = (d, h - 1, s, d) if h == 1 else (d, h - 1, s)
        return pltpu.make_async_remote_copy(
            src_ref=send_buf.at[there],
            dst_ref=recv_buf.at[there],
            send_sem=zout_send.at[d, h - 1, s],
            recv_sem=zout_recv.at[d, h - 1, s],
            device_id=dev(x, at_z(sign)),
            device_id_type=MESH,
        )

    def pick(n, rels):
        rel = rels[-1]
        for m in range(len(rels) - 2, -1, -1):
            rel = jnp.where(n <= m, rels[m], rel)
        return rel

    def z_out_hop(h):
        def step(n, _):
            s = at_x(pick(n, (2, 1, 3, 0)))
            for d in (0, 1):
                sign = 1 - 2 * d
                owner = at_z(sign * (half + 1 - h))
                if h > 1:
                    z_out(d, h - 1, s).wait_recv()
                for w in (d,) if h == 1 else (0, 1):
                    for b in range(per):
                        sums = part(w, owner, s, b)
                        if h > 2 or (h == 2 and w == d):
                            sums = sums + recv_buf[d, h - 2, s, w, b].astype(F32)
                        send_buf[d, h - 1, s, w, b] = sums.astype(BF16)
                z_out(d, h, s).start()
            return 0

        lax.fori_loop(0, NX, step, 0)

    def z_out_last():
        def step(n, _):
            s = at_x(pick(n, (2, 1, 3, 0)))
            for d in (0, 1):
                z_out(d, half, s).wait_recv()
            for w in (0, 1):
                for b in range(per):
                    sums = part(w, z, s, b)
                    for d in (0, 1):
                        sums = sums + recv_buf[d, half - 1, s, w, b].astype(F32)
                    fin[w, pl.ds(pl.multiple_of(s * rows + b * C, C), C)] = sums.astype(BF16)
            for m, r in enumerate((2, 1, 3)):

                @pl.when(n == m)
                def _():
                    for a in (2, 3):
                        x_out(a, r).start()

            return 0

        lax.fori_loop(0, NX, step, 0)
        for a in (2, 3):
            local_out(a).start()

    scale = HD**-0.5
    lane = lax.broadcasted_iota(jnp.int32, (1, HD), 1)
    row = lax.broadcasted_iota(jnp.int32, (W, HD), 0)

    def nt(a, b):
        return lax.dot_general(a, b, (((1,), (1,)), ((), ())), preferred_element_type=F32)

    def tn(a, b):
        return lax.dot_general(a, b, (((0,), (0,)), ((), ())), preferred_element_type=F32)

    def window(w, at):
        found = [kv[w, inv_ref[0, jnp.maximum(at - (NB - 1) + o, 0)]] for o in range(NB)]
        return jnp.concatenate(found, axis=0)

    def stacked(ref, mine):
        return jnp.concatenate([ref[mine, h * HD : (h + 1) * HD] for h in range(GH)], axis=0)

    def unstack(ref, mine, value):
        for h in range(GH):
            ref[mine, h * HD : (h + 1) * HD] = value[h * C : (h + 1) * C]

    def block(i):
        at = place(i)
        mine = pl.ds(pl.multiple_of(i * C, C), C)
        pos = at * C + lax.rem(lane, C)
        first = jnp.zeros_like(pos)
        for end in ends:
            first = jnp.where(pos >= end, end, first)
        t = row + (at - (NB - 1)) * C
        seen = jnp.logical_and(t >= first, t <= pos)
        seen = jnp.concatenate([seen] * (GH * C // HD), axis=1)
        key, val = window(0, at), window(1, at)
        query, grad = stacked(qx, mine), stacked(dx, mine)
        scores = jnp.where(seen, nt(key, query), -jnp.inf)
        peak = jnp.max(scores, axis=0, keepdims=True)
        weights = jnp.exp2((scores - peak) * (scale * LOG2E))
        probs = weights * (1.0 / jnp.sum(weights, axis=0, keepdims=True))
        low = probs.astype(BF16)
        unstack(ox, mine, tn(val, low).T.astype(BF16))
        grad_probs = nt(val, grad)
        centre = jnp.sum(probs * grad_probs, axis=0, keepdims=True)
        grad_scores = (probs * (grad_probs - centre)).astype(BF16)
        unstack(gx, mine, (tn(key, grad_scores) * scale).T.astype(BF16))
        key_grad = jnp.dot(grad_scores, query, preferred_element_type=F32) * scale
        val_grad = jnp.dot(low, grad, preferred_element_type=F32)
        ck[i, pl.ds(1, NB)] = key_grad.reshape(NB, C, HD)
        cv[i, pl.ds(1, NB)] = val_grad.reshape(NB, C, HD)

    came = (1, 3, 0, 2)

    def step(n, _):
        for m, r in enumerate(came):
            if r > 0:

                @pl.when(n == m * per)
                def _():
                    for a in (2, 3):
                        x_in_wait(a, r)

        block(at_x(-pick(n // per, came)) * per + lax.rem(n, per))
        for m, r in enumerate(came):
            if r > 0:

                @pl.when(n == (m + 1) * per - 1)
                def _():
                    for a in (0, 1):
                        x_out(a, NX - r).start()

        return 0

    lax.fori_loop(0, NX * per, step, 0)
    for a in (0, 1):
        local_out(a).start()
    for h in range(1, half + 1):
        z_out_hop(h)
    z_out_last()

    for a in range(4):
        local_out(a).wait()
        for r in (1, 2, 3):
            x_out_wait(a, r)
            x_out(a, r).wait_send()
            x_in(a, r).wait_send()
    for d in (0, 1):
        for h in range(1, half + 1):
            for s in range(NX):
                z_in(d, h, s).wait_send()
                z_out(d, h, s).wait_send()


def settle(*refs):
    srcs, dsts, bufs, sem = refs[:4], refs[4:8], refs[8:12], refs[12]
    copies = []
    for n, (src, dst, buf) in enumerate(zip(srcs, dsts, bufs)):
        parts = 4 if n < 2 else 1
        count = src.shape[0] // parts
        for m in range(parts):
            there = pl.ds(m * count, count)
            copies.append(
                (
                    pltpu.make_async_copy(src.at[there], buf.at[there], sem.at[0, n * 4 + m]),
                    pltpu.make_async_copy(buf.at[there], dst.at[there], sem.at[1, n * 4 + m]),
                )
            )
    for into, _ in copies:
        into.start()
    for into, out in copies:
        into.wait()
        out.start()
    for _, out in copies:
        out.wait()


def local(queries, keys, values, output_gradient, doc_lengths, span_order):
    nz = lax.axis_size("ctx") // NX
    half = nz // 2
    rows = queries.shape[0]
    per = rows // C
    blocks = per * NX * nz
    hbm = pl.BlockSpec(memory_space=pl.ANY)
    smem = pl.BlockSpec(memory_space=pltpu.SMEM)
    dma = pltpu.SemaphoreType.DMA
    outs = (
        jax.ShapeDtypeStruct(queries.shape, BF16),
        jax.ShapeDtypeStruct(queries.shape, BF16),
        jax.ShapeDtypeStruct(keys.shape, BF16),
        jax.ShapeDtypeStruct(keys.shape, BF16),
    )
    results = pl.pallas_call(
        functools.partial(kernel, nz),
        out_shape=outs,
        in_specs=[hbm] * 4 + [smem] * 2,
        out_specs=(hbm,) * 4,
        scratch_shapes=[
            pltpu.VMEM((2, blocks, C, HD), BF16),
            pltpu.VMEM((NX * rows, GW), BF16),
            pltpu.VMEM((NX * rows, GW), BF16),
            pltpu.VMEM((NX * rows, GW), BF16),
            pltpu.VMEM((NX * rows, GW), BF16),
            pltpu.VMEM((NX * per, NB + 2, C, HD), F32),
            pltpu.VMEM((NX * per, NB + 2, C, HD), F32),
            pltpu.VMEM((2, half, NX, 2, per, C, HD), BF16),
            pltpu.VMEM((2, half, NX, 2, per, C, HD), BF16),
            pltpu.VMEM((2, NX * rows, HD), BF16),
            pltpu.VMEM((8, 128), jnp.int32),
            pltpu.SMEM((8, 128), jnp.int32),
            dma((9,)),
            dma((4, 3)),
            dma((4, 3)),
            dma((2, half, NX)),
            dma((2, half, NX)),
            dma((4, 3)),
            dma((4, 3)),
            dma((2, half, NX)),
            dma((2, half, NX)),
        ],
        compiler_params=pltpu.CompilerParams(
            collective_id=0, has_side_effects=True, vmem_limit_bytes=56 * 2**20
        ),
    )(
        queries,
        keys.reshape(per, C, KH * HD),
        values.reshape(per, C, KH * HD),
        output_gradient,
        doc_lengths,
        span_order,
    )
    return pl.pallas_call(
        settle,
        out_shape=outs,
        in_specs=[hbm] * 4,
        out_specs=(hbm,) * 4,
        scratch_shapes=[pltpu.VMEM(o.shape, o.dtype) for o in outs] + [dma((2, 16))],
    )(*results)


def solution(mesh):
    wide = P(("dp", "ctx"), None)
    return jax.shard_map(
        local,
        mesh=mesh,
        in_specs=(wide, wide, wide, wide, P("dp"), P("dp")),
        out_specs=(wide, wide, wide, wide),
        check_vma=False,
    )
```

```python
import functools

import jax
import jax.numpy as jnp
from jax import lax
from jax.experimental import pallas as pl
from jax.experimental.pallas import tpu as pltpu
from jax.sharding import PartitionSpec as P

HD = 128
QH = 32
KH = 4
GH = QH // KH
C = 64
NB = 7
W = NB * C
NX = 4
GW = GH * HD
LOG2E = 1.4426950408889634
STAGES = 8
LAG = 3
MESH = pl.DeviceIdType.MESH
F32 = jnp.float32
BF16 = jnp.bfloat16


def kernel(
    nz,
    q_ref,
    k_ref,
    v_ref,
    g_ref,
    len_ref,
    span_ref,
    o_out,
    gq_out,
    gk_out,
    gv_out,
    kv,
    qx,
    dx,
    ox,
    gx,
    ck,
    cv,
    send_buf,
    recv_buf,
    fin,
    inv_row,
    inv_ref,
    loc_sem,
    xin_send,
    xin_recv,
    zin_send,
    zin_recv,
    xout_send,
    xout_recv,
    zout_send,
    zout_recv,
):
    half = nz // 2
    rows = q_ref.shape[0]
    per = rows // C
    blocks = kv.shape[1]
    me = lax.axis_index("ctx")
    x = me // nz
    z = lax.rem(me, nz)

    def at_x(r):
        return lax.rem(x + r + NX, NX)

    def at_z(r):
        return lax.rem(z + r + nz, nz)

    def dev(xx, zz):
        return {"ctx": xx * nz + zz}

    def cols(g, width):
        return pl.ds(pl.multiple_of(g * width, width), width)

    def pblocks(piece):
        return pl.ds(piece * per, per)

    def prows(piece):
        return pl.ds(pl.multiple_of(piece * rows, rows), rows)

    own = z * NX + x
    local = [
        pltpu.make_async_copy(k_ref.at[:, :, cols(x, HD)], kv.at[0, pblocks(own)], loc_sem.at[0]),
        pltpu.make_async_copy(v_ref.at[:, :, cols(x, HD)], kv.at[1, pblocks(own)], loc_sem.at[1]),
        pltpu.make_async_copy(q_ref.at[:, cols(x, GW)], qx.at[prows(x)], loc_sem.at[2]),
        pltpu.make_async_copy(g_ref.at[:, cols(x, GW)], dx.at[prows(x)], loc_sem.at[3]),
    ]
    for c in local:
        c.start()

    barrier = pltpu.get_barrier_semaphore()
    peers = [dev(at_x(r), z) for r in (1, 2, 3)] + [dev(x, at_z(r)) for r in (1, -1)]
    for p in peers:
        pl.semaphore_signal(barrier, inc=1, device_id=p, device_id_type=MESH)
    pl.semaphore_wait(barrier, len(peers))

    def x_in(a, r):
        g = at_x(r)
        if a < 2:
            src, dst = (k_ref, v_ref)[a].at[:, :, cols(g, HD)], kv.at[a, pblocks(own)]
        else:
            src, dst = (q_ref, g_ref)[a - 2].at[:, cols(g, GW)], (qx, dx)[a - 2].at[prows(x)]
        return pltpu.make_async_remote_copy(
            src_ref=src,
            dst_ref=dst,
            send_sem=xin_send.at[a, r - 1],
            recv_sem=xin_recv.at[a, r - 1],
            device_id=dev(g, z),
            device_id_type=MESH,
        )

    def x_in_wait(a, r):
        src = at_x(-r)
        if a < 2:
            dst = kv.at[a, pblocks(z * NX + src)]
        else:
            dst = (qx, dx)[a - 2].at[prows(src)]
        pltpu.make_async_remote_copy(
            src_ref=dst,
            dst_ref=dst,
            send_sem=xin_send.at[a, r - 1],
            recv_sem=xin_recv.at[a, r - 1],
            device_id=dev(x, z),
            device_id_type=MESH,
        ).wait_recv()

    def z_in_ref(d, h, piece):
        return kv.at[:, pblocks(piece)] if h < half else kv.at[d, pblocks(piece)]

    def z_in(d, h, s):
        sign = 1 - 2 * d
        ref = z_in_ref(d, h, at_z(-sign * (h - 1)) * NX + s)
        return pltpu.make_async_remote_copy(
            src_ref=ref,
            dst_ref=ref,
            send_sem=zin_send.at[d, h - 1, s],
            recv_sem=zin_recv.at[d, h - 1, s],
            device_id=dev(x, at_z(sign)),
            device_id_type=MESH,
        )

    def z_in_wait(d, h, s):
        sign = 1 - 2 * d
        ref = z_in_ref(d, h, at_z(-sign * h) * NX + s)
        pltpu.make_async_remote_copy(
            src_ref=ref,
            dst_ref=ref,
            send_sem=zin_send.at[d, h - 1, s],
            recv_sem=zin_recv.at[d, h - 1, s],
            device_id=dev(x, z),
            device_id_type=MESH,
        ).wait_recv()

    order = (0, 1, 3, 2)

    for r in (1, 3, 2):
        for a in (0, 1):
            x_in(a, r).start()
    local[0].wait()
    local[1].wait()
    for d in (0, 1):
        z_in(d, 1, x).start()
    for r in order[1:]:
        for a in (2, 3):
            x_in(a, r).start()

    at_lane = lax.broadcasted_iota(jnp.int32, inv_row.shape, 1)
    inverse = jnp.zeros(inv_row.shape, jnp.int32)
    for j in range(blocks):
        owner = j // per
        inverse = jnp.where(
            at_lane == span_ref[j], ((owner % nz) * NX + owner // nz) * per + j % per, inverse
        )
    inv_row[...] = inverse
    look = pltpu.make_async_copy(inv_row, inv_ref, loc_sem.at[8])
    look.start()

    def z_in_first(r):
        for a in (0, 1):
            x_in_wait(a, r)
        for d in (0, 1):
            z_in(d, 1, at_x(-r)).start()

    def z_in_pass(h, r):
        for d in (0, 1):
            z_in_wait(d, h, at_x(-r))
            if h < half:
                z_in(d, h + 1, at_x(-r)).start()

    z_in_pass(1, 0)
    z_in_first(1)
    z_in_first(3)
    z_in_pass(2, 0)
    z_in_first(2)

    ends = []
    total = 0
    for n in range(len_ref.shape[0]):
        total = total + len_ref[n]
        ends.append(total)

    zero = jnp.zeros((C, HD), F32)
    for i in range(NX * per):
        for end in (0, NB + 1):
            ck[i, end] = zero
            cv[i, end] = zero

    for h in range(1, half + 1):
        for r in order:
            if r > 0 or h > 2:
                z_in_pass(h, r)
    look.wait()
    local[2].wait()
    local[3].wait()

    def place(i):
        s, b = i // per, lax.rem(i, per)
        return span_ref[(s * nz + z) * per + b]

    def x_out(a, r):
        t = at_x(r)
        if a < 2:
            src, dst = (ox, gx)[a].at[prows(t)], (o_out, gq_out)[a].at[:, cols(x, GW)]
        else:
            src, dst = fin.at[a - 2, prows(t)], (gk_out, gv_out)[a - 2].at[:, cols(x, HD)]
        return pltpu.make_async_remote_copy(
            src_ref=src,
            dst_ref=dst,
            send_sem=xout_send.at[a, r - 1],
            recv_sem=xout_recv.at[a, r - 1],
            device_id=dev(t, z),
            device_id_type=MESH,
        )

    def x_out_wait(a, r):
        src = at_x(-r)
        if a < 2:
            dst = (o_out, gq_out)[a].at[:, cols(src, GW)]
        else:
            dst = (gk_out, gv_out)[a - 2].at[:, cols(src, HD)]
        pltpu.make_async_remote_copy(
            src_ref=dst,
            dst_ref=dst,
            send_sem=xout_send.at[a, r - 1],
            recv_sem=xout_recv.at[a, r - 1],
            device_id=dev(x, z),
            device_id_type=MESH,
        ).wait_recv()

    def local_out(a):
        if a < 2:
            src, dst = (ox, gx)[a].at[prows(x)], (o_out, gq_out)[a].at[:, cols(x, GW)]
        else:
            src, dst = fin.at[a - 2, prows(x)], (gk_out, gv_out)[a - 2].at[:, cols(x, HD)]
        return pltpu.make_async_copy(src, dst, loc_sem.at[4 + a])

    def part(w, zz, s, b):
        at = span_ref[(s * nz + zz) * per + b]
        out = None
        for i in range(NX * per):
            o = jnp.minimum(jnp.maximum(at - place(i) + NB, 0), NB + 1)
            term = (ck, cv)[w][i, o]
            out = term if out is None else out + term
        return out

    def z_out(d, h, s):
        sign = 1 - 2 * d
        there = (d, h - 1, s, d) if h == 1 else (d, h - 1, s)
        return pltpu.make_async_remote_copy(
            src_ref=send_buf.at[there],
            dst_ref=recv_buf.at[there],
            send_sem=zout_send.at[d, h - 1, s],
            recv_sem=zout_recv.at[d, h - 1, s],
            device_id=dev(x, at_z(sign)),
            device_id_type=MESH,
        )

    def pick(n, rels):
        rel = rels[-1]
        for m in range(len(rels) - 2, -1, -1):
            rel = jnp.where(n <= m, rels[m], rel)
        return rel

    def z_out_hop(h):
        def step(n, _):
            s = at_x(pick(n, (2, 1, 3, 0)))
            for d in (0, 1):
                sign = 1 - 2 * d
                owner = at_z(sign * (half + 1 - h))
                if h > 1:
                    z_out(d, h - 1, s).wait_recv()
                for w in (d,) if h == 1 else (0, 1):
                    for b in range(per):
                        sums = part(w, owner, s, b)
                        if h > 2 or (h == 2 and w == d):
                            sums = sums + recv_buf[d, h - 2, s, w, b].astype(F32)
                        send_buf[d, h - 1, s, w, b] = sums.astype(BF16)
                z_out(d, h, s).start()
            return 0

        lax.fori_loop(0, NX, step, 0)

    def z_out_last():
        def step(n, _):
            s = at_x(pick(n, (2, 1, 3, 0)))
            for d in (0, 1):
                z_out(d, half, s).wait_recv()
            for w in (0, 1):
                for b in range(per):
                    sums = part(w, z, s, b)
                    for d in (0, 1):
                        sums = sums + recv_buf[d, half - 1, s, w, b].astype(F32)
                    fin[w, pl.ds(pl.multiple_of(s * rows + b * C, C), C)] = sums.astype(BF16)
            for m, r in enumerate((2, 1, 3)):

                @pl.when(n == m)
                def _():
                    for a in (2, 3):
                        x_out(a, r).start()

            return 0

        lax.fori_loop(0, NX, step, 0)
        for a in (2, 3):
            local_out(a).start()

    scale = HD**-0.5
    lane = lax.broadcasted_iota(jnp.int32, (1, HD), 1)
    row = lax.broadcasted_iota(jnp.int32, (W, HD), 0)

    def nt(a, b):
        return lax.dot_general(a, b, (((1,), (1,)), ((), ())), preferred_element_type=F32)

    def tn(a, b):
        return lax.dot_general(a, b, (((0,), (0,)), ((), ())), preferred_element_type=F32)

    def window(w, at):
        found = [kv[w, inv_ref[0, jnp.maximum(at - (NB - 1) + o, 0)]] for o in range(NB)]
        return jnp.concatenate(found, axis=0)

    def stacked(ref, mine):
        return jnp.concatenate([ref[mine, h * HD : (h + 1) * HD] for h in range(GH)], axis=0)

    def unstack(ref, mine, value):
        for h in range(GH):
            ref[mine, h * HD : (h + 1) * HD] = value[h * C : (h + 1) * C]

    def block(i):
        at = place(i)
        mine = pl.ds(pl.multiple_of(i * C, C), C)
        pos = at * C + lax.rem(lane, C)
        first = jnp.zeros_like(pos)
        for end in ends:
            first = jnp.where(pos >= end, end, first)
        t = row + (at - (NB - 1)) * C
        seen = jnp.logical_and(t >= first, t <= pos)
        seen = jnp.concatenate([seen] * (GH * C // HD), axis=1)
        key, val = window(0, at), window(1, at)
        query, grad = stacked(qx, mine), stacked(dx, mine)
        scores = nt(key, query)
        yield
        grad_probs = nt(val, grad)
        yield
        scores = jnp.where(seen, scores, -jnp.inf)
        peak = jnp.max(scores, axis=0, keepdims=True)
        weights = jnp.exp2((scores - peak) * (scale * LOG2E))
        probs = weights * (1.0 / jnp.sum(weights, axis=0, keepdims=True))
        low = probs.astype(BF16)
        yield
        val_grad = jnp.dot(low, grad, preferred_element_type=F32)
        cv[i, pl.ds(1, NB)] = val_grad.reshape(NB, C, HD)
        yield
        unstack(ox, mine, tn(val, low).T.astype(BF16))
        yield
        centre = jnp.sum(probs * grad_probs, axis=0, keepdims=True)
        grad_scores = (probs * (grad_probs - centre)).astype(BF16)
        yield
        unstack(gx, mine, (tn(key, grad_scores) * scale).T.astype(BF16))
        yield
        key_grad = jnp.dot(grad_scores, query, preferred_element_type=F32) * scale
        ck[i, pl.ds(1, NB)] = key_grad.reshape(NB, C, HD)

    def group(src):
        todo = [block(src * per + b) for b in range(per)]
        for t in range(STAGES + LAG * (per - 1)):
            for b in range(per):
                if t >= LAG * b:
                    next(todo[b], None)

    came = (1, 3, 0, 2)

    def step(n, _):
        for m, r in enumerate(came):
            if r > 0:

                @pl.when(n == m)
                def _():
                    for a in (2, 3):
                        x_in_wait(a, r)

        group(at_x(-pick(n, came)))
        for m, r in enumerate(came):
            if r > 0:

                @pl.when(n == m)
                def _():
                    for a in (0, 1):
                        x_out(a, NX - r).start()

        return 0

    lax.fori_loop(0, NX, step, 0)
    for a in (0, 1):
        local_out(a).start()
    for h in range(1, half + 1):
        z_out_hop(h)
    z_out_last()

    for a in range(4):
        local_out(a).wait()
        for r in (1, 2, 3):
            x_out_wait(a, r)
            x_out(a, r).wait_send()
            x_in(a, r).wait_send()
    for d in (0, 1):
        for h in range(1, half + 1):
            for s in range(NX):
                z_in(d, h, s).wait_send()
                z_out(d, h, s).wait_send()


def settle(*refs):
    srcs, dsts, bufs, sem = refs[:4], refs[4:8], refs[8:12], refs[12]
    copies = []
    for n, (src, dst, buf) in enumerate(zip(srcs, dsts, bufs)):
        parts = 4 if n < 2 else 1
        count = src.shape[0] // parts
        for m in range(parts):
            there = pl.ds(m * count, count)
            copies.append(
                (
                    pltpu.make_async_copy(src.at[there], buf.at[there], sem.at[0, n * 4 + m]),
                    pltpu.make_async_copy(buf.at[there], dst.at[there], sem.at[1, n * 4 + m]),
                )
            )
    for into, _ in copies:
        into.start()
    for into, out in copies:
        into.wait()
        out.start()
    for _, out in copies:
        out.wait()


def local(queries, keys, values, output_gradient, doc_lengths, span_order):
    nz = lax.axis_size("ctx") // NX
    half = nz // 2
    rows = queries.shape[0]
    per = rows // C
    blocks = per * NX * nz
    hbm = pl.BlockSpec(memory_space=pl.ANY)
    smem = pl.BlockSpec(memory_space=pltpu.SMEM)
    dma = pltpu.SemaphoreType.DMA
    outs = (
        jax.ShapeDtypeStruct(queries.shape, BF16),
        jax.ShapeDtypeStruct(queries.shape, BF16),
        jax.ShapeDtypeStruct(keys.shape, BF16),
        jax.ShapeDtypeStruct(keys.shape, BF16),
    )
    results = pl.pallas_call(
        functools.partial(kernel, nz),
        out_shape=outs,
        in_specs=[hbm] * 4 + [smem] * 2,
        out_specs=(hbm,) * 4,
        scratch_shapes=[
            pltpu.VMEM((2, blocks, C, HD), BF16),
            pltpu.VMEM((NX * rows, GW), BF16),
            pltpu.VMEM((NX * rows, GW), BF16),
            pltpu.VMEM((NX * rows, GW), BF16),
            pltpu.VMEM((NX * rows, GW), BF16),
            pltpu.VMEM((NX * per, NB + 2, C, HD), F32),
            pltpu.VMEM((NX * per, NB + 2, C, HD), F32),
            pltpu.VMEM((2, half, NX, 2, per, C, HD), BF16),
            pltpu.VMEM((2, half, NX, 2, per, C, HD), BF16),
            pltpu.VMEM((2, NX * rows, HD), BF16),
            pltpu.VMEM((8, 128), jnp.int32),
            pltpu.SMEM((8, 128), jnp.int32),
            dma((9,)),
            dma((4, 3)),
            dma((4, 3)),
            dma((2, half, NX)),
            dma((2, half, NX)),
            dma((4, 3)),
            dma((4, 3)),
            dma((2, half, NX)),
            dma((2, half, NX)),
        ],
        compiler_params=pltpu.CompilerParams(
            collective_id=0, has_side_effects=True, vmem_limit_bytes=56 * 2**20
        ),
    )(
        queries,
        keys.reshape(per, C, KH * HD),
        values.reshape(per, C, KH * HD),
        output_gradient,
        doc_lengths,
        span_order,
    )
    return pl.pallas_call(
        settle,
        out_shape=outs,
        in_specs=[hbm] * 4,
        out_specs=(hbm,) * 4,
        scratch_shapes=[pltpu.VMEM(o.shape, o.dtype) for o in outs] + [dma((2, 16))],
    )(*results)


def solution(mesh):
    wide = P(("dp", "ctx"), None)
    return jax.shard_map(
        local,
        mesh=mesh,
        in_specs=(wide, wide, wide, wide, P("dp"), P("dp")),
        out_specs=(wide, wide, wide, wide),
        check_vma=False,
    )
```

```python
import functools

import jax
import jax.numpy as jnp
from jax import lax
from jax.experimental import pallas as pl
from jax.experimental.pallas import tpu as pltpu
from jax.sharding import PartitionSpec as P

HD = 128
QH = 32
KH = 4
GH = QH // KH
C = 64
NB = 7
W = NB * C
NX = 4
GW = GH * HD
LOG2E = 1.4426950408889634
STAGES = 8
LAG = 3
MESH = pl.DeviceIdType.MESH
F32 = jnp.float32
BF16 = jnp.bfloat16


def kernel(
    nz,
    q_ref,
    k_ref,
    v_ref,
    g_ref,
    len_hbm,
    span_hbm,
    o_out,
    gq_out,
    gk_out,
    gv_out,
    kv,
    qx,
    dx,
    ox,
    gx,
    ck,
    cv,
    send_buf,
    recv_buf,
    fin,
    len_ref,
    span_ref,
    inv_row,
    inv_ref,
    loc_sem,
    xin_send,
    xin_recv,
    zin_send,
    zin_recv,
    xout_send,
    xout_recv,
    zout_send,
    zout_recv,
):
    half = nz // 2
    rows = q_ref.shape[0]
    per = rows // C
    blocks = kv.shape[1]
    me = lax.axis_index("ctx")
    x = me // nz
    z = lax.rem(me, nz)

    def at_x(r):
        return lax.rem(x + r + NX, NX)

    def at_z(r):
        return lax.rem(z + r + nz, nz)

    def dev(xx, zz):
        return {"ctx": xx * nz + zz}

    def cols(g, width):
        return pl.ds(pl.multiple_of(g * width, width), width)

    def pblocks(piece):
        return pl.ds(piece * per, per)

    def prows(piece):
        return pl.ds(pl.multiple_of(piece * rows, rows), rows)

    own = z * NX + x
    local = [
        pltpu.make_async_copy(k_ref.at[:, :, cols(x, HD)], kv.at[0, pblocks(own)], loc_sem.at[0]),
        pltpu.make_async_copy(v_ref.at[:, :, cols(x, HD)], kv.at[1, pblocks(own)], loc_sem.at[1]),
        pltpu.make_async_copy(q_ref.at[:, cols(x, GW)], qx.at[prows(x)], loc_sem.at[2]),
        pltpu.make_async_copy(g_ref.at[:, cols(x, GW)], dx.at[prows(x)], loc_sem.at[3]),
    ]
    local.append(pltpu.make_async_copy(len_hbm, len_ref, loc_sem.at[9]))
    local.append(pltpu.make_async_copy(span_hbm, span_ref, loc_sem.at[10]))
    for c in local:
        c.start()

    barrier = pltpu.get_barrier_semaphore()
    peers = [dev(at_x(r), z) for r in (1, 2, 3)] + [dev(x, at_z(r)) for r in (1, -1)]
    for p in peers:
        pl.semaphore_signal(barrier, inc=1, device_id=p, device_id_type=MESH)
    pl.semaphore_wait(barrier, len(peers))

    def x_in(a, r):
        g = at_x(r)
        if a < 2:
            src, dst = (k_ref, v_ref)[a].at[:, :, cols(g, HD)], kv.at[a, pblocks(own)]
        else:
            src, dst = (q_ref, g_ref)[a - 2].at[:, cols(g, GW)], (qx, dx)[a - 2].at[prows(x)]
        return pltpu.make_async_remote_copy(
            src_ref=src,
            dst_ref=dst,
            send_sem=xin_send.at[a, r - 1],
            recv_sem=xin_recv.at[a, r - 1],
            device_id=dev(g, z),
            device_id_type=MESH,
        )

    def x_in_wait(a, r):
        src = at_x(-r)
        if a < 2:
            dst = kv.at[a, pblocks(z * NX + src)]
        else:
            dst = (qx, dx)[a - 2].at[prows(src)]
        pltpu.make_async_remote_copy(
            src_ref=dst,
            dst_ref=dst,
            send_sem=xin_send.at[a, r - 1],
            recv_sem=xin_recv.at[a, r - 1],
            device_id=dev(x, z),
            device_id_type=MESH,
        ).wait_recv()

    def z_in_ref(d, h, piece):
        return kv.at[:, pblocks(piece)] if h < half else kv.at[d, pblocks(piece)]

    def z_in(d, h, s):
        sign = 1 - 2 * d
        ref = z_in_ref(d, h, at_z(-sign * (h - 1)) * NX + s)
        return pltpu.make_async_remote_copy(
            src_ref=ref,
            dst_ref=ref,
            send_sem=zin_send.at[d, h - 1, s],
            recv_sem=zin_recv.at[d, h - 1, s],
            device_id=dev(x, at_z(sign)),
            device_id_type=MESH,
        )

    def z_in_wait(d, h, s):
        sign = 1 - 2 * d
        ref = z_in_ref(d, h, at_z(-sign * h) * NX + s)
        pltpu.make_async_remote_copy(
            src_ref=ref,
            dst_ref=ref,
            send_sem=zin_send.at[d, h - 1, s],
            recv_sem=zin_recv.at[d, h - 1, s],
            device_id=dev(x, z),
            device_id_type=MESH,
        ).wait_recv()

    order = (0, 1, 3, 2)

    for r in (1, 3, 2):
        for a in (0, 1):
            x_in(a, r).start()
    local[0].wait()
    local[1].wait()
    for d in (0, 1):
        z_in(d, 1, x).start()
    for r in order[1:]:
        for a in (2, 3):
            x_in(a, r).start()

    local[4].wait()
    local[5].wait()
    at_lane = lax.broadcasted_iota(jnp.int32, inv_row.shape, 1)
    inverse = jnp.zeros(inv_row.shape, jnp.int32)
    for j in range(blocks):
        owner = j // per
        inverse = jnp.where(
            at_lane == span_ref[j], ((owner % nz) * NX + owner // nz) * per + j % per, inverse
        )
    inv_row[...] = inverse
    look = pltpu.make_async_copy(inv_row, inv_ref, loc_sem.at[8])
    look.start()

    def z_in_first(r):
        for a in (0, 1):
            x_in_wait(a, r)
        for d in (0, 1):
            z_in(d, 1, at_x(-r)).start()

    def z_in_pass(h, r):
        for d in (0, 1):
            z_in_wait(d, h, at_x(-r))
            if h < half:
                z_in(d, h + 1, at_x(-r)).start()

    z_in_pass(1, 0)
    z_in_first(1)
    z_in_first(3)
    z_in_pass(2, 0)
    z_in_first(2)

    ends = []
    total = 0
    for n in range(len_ref.shape[0]):
        total = total + len_ref[n]
        ends.append(total)

    zero = jnp.zeros((C, HD), F32)
    for i in range(NX * per):
        for end in (0, NB + 1):
            ck[i, end] = zero
            cv[i, end] = zero

    for h in range(1, half + 1):
        for r in order:
            if r > 0 or h > 2:
                z_in_pass(h, r)
    look.wait()
    local[2].wait()
    local[3].wait()

    def place(i):
        s, b = i // per, lax.rem(i, per)
        return span_ref[(s * nz + z) * per + b]

    def x_out(a, r):
        t = at_x(r)
        if a < 2:
            src, dst = (ox, gx)[a].at[prows(t)], (o_out, gq_out)[a].at[:, cols(x, GW)]
        else:
            src, dst = fin.at[a - 2, prows(t)], (gk_out, gv_out)[a - 2].at[:, cols(x, HD)]
        return pltpu.make_async_remote_copy(
            src_ref=src,
            dst_ref=dst,
            send_sem=xout_send.at[a, r - 1],
            recv_sem=xout_recv.at[a, r - 1],
            device_id=dev(t, z),
            device_id_type=MESH,
        )

    def x_out_wait(a, r):
        src = at_x(-r)
        if a < 2:
            dst = (o_out, gq_out)[a].at[:, cols(src, GW)]
        else:
            dst = (gk_out, gv_out)[a - 2].at[:, cols(src, HD)]
        pltpu.make_async_remote_copy(
            src_ref=dst,
            dst_ref=dst,
            send_sem=xout_send.at[a, r - 1],
            recv_sem=xout_recv.at[a, r - 1],
            device_id=dev(x, z),
            device_id_type=MESH,
        ).wait_recv()

    def local_out(a):
        if a < 2:
            src, dst = (ox, gx)[a].at[prows(x)], (o_out, gq_out)[a].at[:, cols(x, GW)]
        else:
            src, dst = fin.at[a - 2, prows(x)], (gk_out, gv_out)[a - 2].at[:, cols(x, HD)]
        return pltpu.make_async_copy(src, dst, loc_sem.at[4 + a])

    def part(w, zz, s, b):
        at = span_ref[(s * nz + zz) * per + b]
        out = None
        for i in range(NX * per):
            o = jnp.minimum(jnp.maximum(at - place(i) + NB, 0), NB + 1)
            term = (ck, cv)[w][i, o]
            out = term if out is None else out + term
        return out

    def z_out(d, h, s):
        sign = 1 - 2 * d
        there = (d, h - 1, s, d) if h == 1 else (d, h - 1, s)
        return pltpu.make_async_remote_copy(
            src_ref=send_buf.at[there],
            dst_ref=recv_buf.at[there],
            send_sem=zout_send.at[d, h - 1, s],
            recv_sem=zout_recv.at[d, h - 1, s],
            device_id=dev(x, at_z(sign)),
            device_id_type=MESH,
        )

    def pick(n, rels):
        rel = rels[-1]
        for m in range(len(rels) - 2, -1, -1):
            rel = jnp.where(n <= m, rels[m], rel)
        return rel

    def z_out_hop(h):
        def step(n, _):
            s = at_x(pick(n, (2, 1, 3, 0)))
            for d in (0, 1):
                sign = 1 - 2 * d
                owner = at_z(sign * (half + 1 - h))
                which = [(w, b) for w in ((d,) if h == 1 else (0, 1)) for b in range(per)]
                parts = [part(w, owner, s, b) for w, b in which]
                if h > 1:
                    z_out(d, h - 1, s).wait_recv()
                for (w, b), sums in zip(which, parts):
                    if h > 2 or (h == 2 and w == d):
                        sums = sums + recv_buf[d, h - 2, s, w, b].astype(F32)
                    send_buf[d, h - 1, s, w, b] = sums.astype(BF16)
                z_out(d, h, s).start()
            return 0

        lax.fori_loop(0, NX, step, 0)

    def z_out_last():
        def step(n, _):
            s = at_x(pick(n, (2, 1, 3, 0)))
            which = [(w, b) for w in (0, 1) for b in range(per)]
            parts = [part(w, z, s, b) for w, b in which]
            for d in (0, 1):
                z_out(d, half, s).wait_recv()
            for (w, b), sums in zip(which, parts):
                for d in (0, 1):
                    sums = sums + recv_buf[d, half - 1, s, w, b].astype(F32)
                fin[w, pl.ds(pl.multiple_of(s * rows + b * C, C), C)] = sums.astype(BF16)
            for m, r in enumerate((2, 1, 3)):

                @pl.when(n == m)
                def _():
                    for a in (2, 3):
                        x_out(a, r).start()

            return 0

        lax.fori_loop(0, NX, step, 0)
        for a in (2, 3):
            local_out(a).start()

    scale = HD**-0.5
    lane = lax.broadcasted_iota(jnp.int32, (1, HD), 1)
    row = lax.broadcasted_iota(jnp.int32, (W, HD), 0)

    def nt(a, b):
        return lax.dot_general(a, b, (((1,), (1,)), ((), ())), preferred_element_type=F32)

    def tn(a, b):
        return lax.dot_general(a, b, (((0,), (0,)), ((), ())), preferred_element_type=F32)

    def window(w, at):
        found = [kv[w, inv_ref[0, jnp.maximum(at - (NB - 1) + o, 0)]] for o in range(NB)]
        return jnp.concatenate(found, axis=0)

    def stacked(ref, mine):
        return jnp.concatenate([ref[mine, h * HD : (h + 1) * HD] for h in range(GH)], axis=0)

    def unstack(ref, mine, value):
        for h in range(GH):
            ref[mine, h * HD : (h + 1) * HD] = value[h * C : (h + 1) * C]

    def block(i):
        at = place(i)
        mine = pl.ds(pl.multiple_of(i * C, C), C)
        pos = at * C + lax.rem(lane, C)
        first = jnp.zeros_like(pos)
        for end in ends:
            first = jnp.where(pos >= end, end, first)
        t = row + (at - (NB - 1)) * C
        seen = jnp.logical_and(t >= first, t <= pos)
        seen = jnp.concatenate([seen] * (GH * C // HD), axis=1)
        key, val = window(0, at), window(1, at)
        query, grad = stacked(qx, mine), stacked(dx, mine)
        scores = nt(key, query)
        yield
        grad_probs = nt(val, grad)
        yield
        scores = jnp.where(seen, scores, -jnp.inf)
        peak = jnp.max(scores, axis=0, keepdims=True)
        weights = jnp.exp2((scores - peak) * (scale * LOG2E))
        probs = weights * (1.0 / jnp.sum(weights, axis=0, keepdims=True))
        low = probs.astype(BF16)
        yield
        val_grad = jnp.dot(low, grad, preferred_element_type=F32)
        cv[i, pl.ds(1, NB)] = val_grad.reshape(NB, C, HD)
        yield
        unstack(ox, mine, tn(val, low).T.astype(BF16))
        yield
        centre = jnp.sum(probs * grad_probs, axis=0, keepdims=True)
        grad_scores = (probs * (grad_probs - centre)).astype(BF16)
        yield
        unstack(gx, mine, (tn(key, grad_scores) * scale).T.astype(BF16))
        yield
        key_grad = jnp.dot(grad_scores, query, preferred_element_type=F32) * scale
        ck[i, pl.ds(1, NB)] = key_grad.reshape(NB, C, HD)

    def group(src):
        todo = [block(src * per + b) for b in range(per)]
        for t in range(STAGES + LAG * (per - 1)):
            for b in range(per):
                if t >= LAG * b:
                    next(todo[b], None)

    came = (1, 3, 0, 2)

    def step(n, _):
        for m, r in enumerate(came):
            if r > 0:

                @pl.when(n == m)
                def _():
                    for a in (2, 3):
                        x_in_wait(a, r)

        group(at_x(-pick(n, came)))
        for m, r in enumerate(came):
            if r > 0:

                @pl.when(n == m)
                def _():
                    for a in (0, 1):
                        x_out(a, NX - r).start()

        return 0

    lax.fori_loop(0, NX, step, 0)
    for a in (0, 1):
        local_out(a).start()
    for h in range(1, half + 1):
        z_out_hop(h)
    z_out_last()

    for a in range(4):
        local_out(a).wait()
        for r in (1, 2, 3):
            x_out_wait(a, r)
            x_out(a, r).wait_send()
            x_in(a, r).wait_send()
    for d in (0, 1):
        for h in range(1, half + 1):
            for s in range(NX):
                z_in(d, h, s).wait_send()
                z_out(d, h, s).wait_send()


def settle(*refs):
    srcs, dsts, sem = refs[:4], refs[4:8], refs[8]
    copies = [
        pltpu.make_async_copy(src, dst, sem.at[n]) for n, (src, dst) in enumerate(zip(srcs, dsts))
    ]
    for c in copies:
        c.start()
    for c in copies:
        c.wait()


def local(queries, keys, values, output_gradient, doc_lengths, span_order):
    nz = lax.axis_size("ctx") // NX
    half = nz // 2
    rows = queries.shape[0]
    per = rows // C
    blocks = per * NX * nz
    hbm = pl.BlockSpec(memory_space=pl.ANY)
    dma = pltpu.SemaphoreType.DMA
    outs = (
        jax.ShapeDtypeStruct(queries.shape, BF16),
        jax.ShapeDtypeStruct(queries.shape, BF16),
        jax.ShapeDtypeStruct(keys.shape, BF16),
        jax.ShapeDtypeStruct(keys.shape, BF16),
    )
    results = pl.pallas_call(
        functools.partial(kernel, nz),
        out_shape=tuple(pltpu.VMEM(o.shape, o.dtype) for o in outs),
        in_specs=[hbm] * 6,
        out_specs=(pl.BlockSpec(memory_space=pltpu.VMEM),) * 4,
        scratch_shapes=[
            pltpu.VMEM((2, blocks, C, HD), BF16),
            pltpu.VMEM((NX * rows, GW), BF16),
            pltpu.VMEM((NX * rows, GW), BF16),
            pltpu.VMEM((NX * rows, GW), BF16),
            pltpu.VMEM((NX * rows, GW), BF16),
            pltpu.VMEM((NX * per, NB + 2, C, HD), F32),
            pltpu.VMEM((NX * per, NB + 2, C, HD), F32),
            pltpu.VMEM((2, half, NX, 2, per, C, HD), BF16),
            pltpu.VMEM((2, half, NX, 2, per, C, HD), BF16),
            pltpu.VMEM((2, NX * rows, HD), BF16),
            pltpu.SMEM(doc_lengths.shape, jnp.int32),
            pltpu.SMEM(span_order.shape, jnp.int32),
            pltpu.VMEM((8, 128), jnp.int32),
            pltpu.SMEM((8, 128), jnp.int32),
            dma((11,)),
            dma((4, 3)),
            dma((4, 3)),
            dma((2, half, NX)),
            dma((2, half, NX)),
            dma((4, 3)),
            dma((4, 3)),
            dma((2, half, NX)),
            dma((2, half, NX)),
        ],
        compiler_params=pltpu.CompilerParams(
            collective_id=0, has_side_effects=True, vmem_limit_bytes=56 * 2**20
        ),
    )(
        queries,
        keys.reshape(per, C, KH * HD),
        values.reshape(per, C, KH * HD),
        output_gradient,
        doc_lengths,
        span_order,
    )
    return pl.pallas_call(
        settle,
        out_shape=outs,
        in_specs=[hbm] * 4,
        out_specs=(hbm,) * 4,
        scratch_shapes=[dma((4,))],
    )(*(pltpu.with_memory_space_constraint(r, pltpu.VMEM) for r in results))


def solution(mesh):
    wide = P(("dp", "ctx"), None)
    return jax.shard_map(
        local,
        mesh=mesh,
        in_specs=(wide, wide, wide, wide, P("dp"), P("dp")),
        out_specs=(wide, wide, wide, wide),
        check_vma=False,
    )
```

```python
import functools

import jax
import jax.numpy as jnp
from jax import lax
from jax.experimental import pallas as pl
from jax.experimental.pallas import tpu as pltpu
from jax.sharding import PartitionSpec as P

HD = 128
QH = 32
KH = 4
GH = QH // KH
C = 64
NB = 7
W = NB * C
NX = 4
GW = GH * HD
LOG2E = 1.4426950408889634
MESH = pl.DeviceIdType.MESH
F32 = jnp.float32
BF16 = jnp.bfloat16


def kernel(
    nz,
    q_ref,
    k_ref,
    v_ref,
    g_ref,
    len_hbm,
    span_hbm,
    o_out,
    gq_out,
    gk_out,
    gv_out,
    kv,
    qx,
    dx,
    ox,
    gx,
    ck,
    cv,
    low_buf,
    score_buf,
    send_buf,
    recv_buf,
    fin,
    len_ref,
    span_ref,
    inv_row,
    inv_ref,
    loc_sem,
    xin_send,
    xin_recv,
    zin_send,
    zin_recv,
    xout_send,
    xout_recv,
    zout_send,
    zout_recv,
):
    half = nz // 2
    rows = q_ref.shape[0]
    per = rows // C
    blocks = kv.shape[1]
    me = lax.axis_index("ctx")
    x = me // nz
    z = lax.rem(me, nz)

    def at_x(r):
        return lax.rem(x + r + NX, NX)

    def at_z(r):
        return lax.rem(z + r + nz, nz)

    def dev(xx, zz):
        return {"ctx": xx * nz + zz}

    def cols(g, width):
        return pl.ds(pl.multiple_of(g * width, width), width)

    def pblocks(piece):
        return pl.ds(piece * per, per)

    def prows(piece):
        return pl.ds(pl.multiple_of(piece * rows, rows), rows)

    own = z * NX + x
    local = [
        pltpu.make_async_copy(k_ref.at[:, :, cols(x, HD)], kv.at[0, pblocks(own)], loc_sem.at[0]),
        pltpu.make_async_copy(v_ref.at[:, :, cols(x, HD)], kv.at[1, pblocks(own)], loc_sem.at[1]),
        pltpu.make_async_copy(q_ref.at[:, cols(x, GW)], qx.at[prows(x)], loc_sem.at[2]),
        pltpu.make_async_copy(g_ref.at[:, cols(x, GW)], dx.at[prows(x)], loc_sem.at[3]),
    ]
    local.append(pltpu.make_async_copy(len_hbm, len_ref, loc_sem.at[9]))
    local.append(pltpu.make_async_copy(span_hbm, span_ref, loc_sem.at[10]))
    for c in local:
        c.start()

    barrier = pltpu.get_barrier_semaphore()
    peers = [dev(at_x(r), z) for r in (1, 2, 3)] + [dev(x, at_z(r)) for r in (1, -1)]
    for p in peers:
        pl.semaphore_signal(barrier, inc=1, device_id=p, device_id_type=MESH)
    pl.semaphore_wait(barrier, len(peers))

    def x_in(a, r):
        g = at_x(r)
        if a < 2:
            src, dst = (k_ref, v_ref)[a].at[:, :, cols(g, HD)], kv.at[a, pblocks(own)]
        else:
            src, dst = (q_ref, g_ref)[a - 2].at[:, cols(g, GW)], (qx, dx)[a - 2].at[prows(x)]
        return pltpu.make_async_remote_copy(
            src_ref=src,
            dst_ref=dst,
            send_sem=xin_send.at[a, r - 1],
            recv_sem=xin_recv.at[a, r - 1],
            device_id=dev(g, z),
            device_id_type=MESH,
        )

    def x_in_wait(a, r):
        src = at_x(-r)
        if a < 2:
            dst = kv.at[a, pblocks(z * NX + src)]
        else:
            dst = (qx, dx)[a - 2].at[prows(src)]
        pltpu.make_async_remote_copy(
            src_ref=dst,
            dst_ref=dst,
            send_sem=xin_send.at[a, r - 1],
            recv_sem=xin_recv.at[a, r - 1],
            device_id=dev(x, z),
            device_id_type=MESH,
        ).wait_recv()

    def z_in_ref(d, h, piece):
        return kv.at[:, pblocks(piece)] if h < half else kv.at[d, pblocks(piece)]

    def z_in(d, h, s):
        sign = 1 - 2 * d
        ref = z_in_ref(d, h, at_z(-sign * (h - 1)) * NX + s)
        return pltpu.make_async_remote_copy(
            src_ref=ref,
            dst_ref=ref,
            send_sem=zin_send.at[d, h - 1, s],
            recv_sem=zin_recv.at[d, h - 1, s],
            device_id=dev(x, at_z(sign)),
            device_id_type=MESH,
        )

    def z_in_wait(d, h, s):
        sign = 1 - 2 * d
        ref = z_in_ref(d, h, at_z(-sign * h) * NX + s)
        pltpu.make_async_remote_copy(
            src_ref=ref,
            dst_ref=ref,
            send_sem=zin_send.at[d, h - 1, s],
            recv_sem=zin_recv.at[d, h - 1, s],
            device_id=dev(x, z),
            device_id_type=MESH,
        ).wait_recv()

    order = (0, 1, 3, 2)

    for r in (1, 3, 2):
        for a in (0, 1):
            x_in(a, r).start()
    local[0].wait()
    local[1].wait()
    for d in (0, 1):
        z_in(d, 1, x).start()
    for r in order[1:]:
        for a in (2, 3):
            x_in(a, r).start()

    local[4].wait()
    local[5].wait()
    at_lane = lax.broadcasted_iota(jnp.int32, inv_row.shape, 1)
    inverse = jnp.zeros(inv_row.shape, jnp.int32)
    for j in range(blocks):
        owner = j // per
        inverse = jnp.where(
            at_lane == span_ref[j], ((owner % nz) * NX + owner // nz) * per + j % per, inverse
        )
    inv_row[...] = inverse
    look = pltpu.make_async_copy(inv_row, inv_ref, loc_sem.at[8])
    look.start()

    def z_in_first(r):
        for a in (0, 1):
            x_in_wait(a, r)
        for d in (0, 1):
            z_in(d, 1, at_x(-r)).start()

    def z_in_pass(h, r):
        for d in (0, 1):
            z_in_wait(d, h, at_x(-r))
            if h < half:
                z_in(d, h + 1, at_x(-r)).start()

    z_in_pass(1, 0)
    z_in_first(1)
    z_in_first(3)
    z_in_pass(2, 0)
    z_in_first(2)

    ends = []
    total = 0
    for n in range(len_ref.shape[0]):
        total = total + len_ref[n]
        ends.append(total)

    zero = jnp.zeros((C, HD), F32)
    for i in range(NX * per):
        for end in (0, NB + 1):
            ck[i, end] = zero
            cv[i, end] = zero

    for h in range(1, half + 1):
        for r in order:
            if r > 0 or h > 2:
                z_in_pass(h, r)
    look.wait()
    local[2].wait()
    local[3].wait()

    def place(i):
        s, b = i // per, lax.rem(i, per)
        return span_ref[(s * nz + z) * per + b]

    def x_out(a, r):
        t = at_x(r)
        if a < 2:
            src, dst = (ox, gx)[a].at[prows(t)], (o_out, gq_out)[a].at[:, cols(x, GW)]
        else:
            src, dst = fin.at[a - 2, prows(t)], (gk_out, gv_out)[a - 2].at[:, cols(x, HD)]
        return pltpu.make_async_remote_copy(
            src_ref=src,
            dst_ref=dst,
            send_sem=xout_send.at[a, r - 1],
            recv_sem=xout_recv.at[a, r - 1],
            device_id=dev(t, z),
            device_id_type=MESH,
        )

    def x_out_wait(a, r):
        src = at_x(-r)
        if a < 2:
            dst = (o_out, gq_out)[a].at[:, cols(src, GW)]
        else:
            dst = (gk_out, gv_out)[a - 2].at[:, cols(src, HD)]
        pltpu.make_async_remote_copy(
            src_ref=dst,
            dst_ref=dst,
            send_sem=xout_send.at[a, r - 1],
            recv_sem=xout_recv.at[a, r - 1],
            device_id=dev(x, z),
            device_id_type=MESH,
        ).wait_recv()

    def local_out(a):
        if a < 2:
            src, dst = (ox, gx)[a].at[prows(x)], (o_out, gq_out)[a].at[:, cols(x, GW)]
        else:
            src, dst = fin.at[a - 2, prows(x)], (gk_out, gv_out)[a - 2].at[:, cols(x, HD)]
        return pltpu.make_async_copy(src, dst, loc_sem.at[4 + a])

    def part(w, zz, s, b):
        at = span_ref[(s * nz + zz) * per + b]
        out = None
        for i in range(NX * per):
            o = jnp.minimum(jnp.maximum(at - place(i) + NB, 0), NB + 1)
            term = (ck, cv)[w][i, o]
            out = term if out is None else out + term
        return out

    def z_out(d, h, s):
        sign = 1 - 2 * d
        there = (d, h - 1, s, d) if h == 1 else (d, h - 1, s)
        return pltpu.make_async_remote_copy(
            src_ref=send_buf.at[there],
            dst_ref=recv_buf.at[there],
            send_sem=zout_send.at[d, h - 1, s],
            recv_sem=zout_recv.at[d, h - 1, s],
            device_id=dev(x, at_z(sign)),
            device_id_type=MESH,
        )

    def pick(n, rels):
        rel = rels[-1]
        for m in range(len(rels) - 2, -1, -1):
            rel = jnp.where(n <= m, rels[m], rel)
        return rel

    def z_out_hop(h):
        def step(n, _):
            s = at_x(pick(n, (2, 1, 3, 0)))
            for d in (0, 1):
                sign = 1 - 2 * d
                owner = at_z(sign * (half + 1 - h))
                which = [(w, b) for w in ((d,) if h == 1 else (0, 1)) for b in range(per)]
                parts = [part(w, owner, s, b) for w, b in which]
                if h > 1:
                    z_out(d, h - 1, s).wait_recv()
                for (w, b), sums in zip(which, parts):
                    if h > 2 or (h == 2 and w == d):
                        sums = sums + recv_buf[d, h - 2, s, w, b].astype(F32)
                    send_buf[d, h - 1, s, w, b] = sums.astype(BF16)
                z_out(d, h, s).start()
            return 0

        lax.fori_loop(0, NX, step, 0)

    def z_out_last():
        def step(n, _):
            s = at_x(pick(n, (2, 1, 3, 0)))
            which = [(w, b) for w in (0, 1) for b in range(per)]
            parts = [part(w, z, s, b) for w, b in which]
            for d in (0, 1):
                z_out(d, half, s).wait_recv()
            for (w, b), sums in zip(which, parts):
                for d in (0, 1):
                    sums = sums + recv_buf[d, half - 1, s, w, b].astype(F32)
                fin[w, pl.ds(pl.multiple_of(s * rows + b * C, C), C)] = sums.astype(BF16)
            for m, r in enumerate((2, 1, 3)):

                @pl.when(n == m)
                def _():
                    for a in (2, 3):
                        x_out(a, r).start()

            return 0

        lax.fori_loop(0, NX, step, 0)
        for a in (2, 3):
            local_out(a).start()

    scale = HD**-0.5
    lane = lax.broadcasted_iota(jnp.int32, (1, HD), 1)
    row = lax.broadcasted_iota(jnp.int32, (W, HD), 0)

    def nt(a, b):
        return lax.dot_general(a, b, (((1,), (1,)), ((), ())), preferred_element_type=F32)

    def tn(a, b):
        return lax.dot_general(a, b, (((0,), (0,)), ((), ())), preferred_element_type=F32)

    def window(w, at):
        found = [kv[w, inv_ref[0, jnp.maximum(at - (NB - 1) + o, 0)]] for o in range(NB)]
        return jnp.concatenate(found, axis=0)

    def stacked(ref, mine):
        return jnp.concatenate([ref[mine, h * HD : (h + 1) * HD] for h in range(GH)], axis=0)

    def unstack(ref, mine, value):
        for h in range(GH):
            ref[mine, h * HD : (h + 1) * HD] = value[h * C : (h + 1) * C]

    def block(i, late):
        at = place(i)
        mine = pl.ds(pl.multiple_of(i * C, C), C)
        pos = at * C + lax.rem(lane, C)
        first = jnp.zeros_like(pos)
        for end in ends:
            first = jnp.where(pos >= end, end, first)
        t = row + (at - (NB - 1)) * C
        seen = jnp.logical_and(t >= first, t <= pos)
        seen = jnp.concatenate([seen] * (GH * C // HD), axis=1)
        key, val = window(0, at), window(1, at)
        query, grad = stacked(qx, mine), stacked(dx, mine)
        scores = nt(key, query)
        yield
        grad_probs = nt(val, grad)
        yield
        scores = jnp.where(seen, scores, -jnp.inf)
        peak = jnp.max(scores, axis=0, keepdims=True)
        weights = jnp.exp2((scores - peak) * (scale * LOG2E))
        probs = weights * (1.0 / jnp.sum(weights, axis=0, keepdims=True))
        low = probs.astype(BF16)
        if late:
            low_buf[i] = low
        yield
        val_grad = jnp.dot(low, grad, preferred_element_type=F32)
        cv[i, pl.ds(1, NB)] = val_grad.reshape(NB, C, HD)
        yield
        if not late:
            unstack(ox, mine, tn(val, low).T.astype(BF16))
            yield
        centre = jnp.sum(probs * grad_probs, axis=0, keepdims=True)
        grad_scores = (probs * (grad_probs - centre)).astype(BF16)
        if late:
            score_buf[i] = grad_scores
        yield
        if not late:
            unstack(gx, mine, (tn(key, grad_scores) * scale).T.astype(BF16))
            yield
        key_grad = jnp.dot(grad_scores, query, preferred_element_type=F32) * scale
        ck[i, pl.ds(1, NB)] = key_grad.reshape(NB, C, HD)

    def finish(i):
        at = place(i)
        mine = pl.ds(pl.multiple_of(i * C, C), C)
        unstack(ox, mine, tn(window(1, at), low_buf[i]).T.astype(BF16))
        yield
        unstack(gx, mine, (tn(window(0, at), score_buf[i]) * scale).T.astype(BF16))

    def group(src, work, lag):
        todo = [work(src * per + b) for b in range(per)]
        busy = [True] * per
        t = 0
        while any(busy):
            for b in range(per):
                if busy[b] and t >= lag * b:
                    busy[b] = next(todo[b], "end") != "end"
            t += 1

    def arrive(n, m, r):
        @pl.when(n == m)
        def _():
            for a in (2, 3):
                x_in_wait(a, r)

    def leave(n, m, r):
        @pl.when(n == m)
        def _():
            for a in (0, 1):
                x_out(a, r).start()

    def near(n, _):
        arrive(n, 0, 1)
        arrive(n, 1, 3)
        group(at_x(-pick(n, (1, 3))), functools.partial(block, late=False), 3)
        leave(n, 0, 3)
        leave(n, 1, 1)
        return 0

    def far(n, _):
        arrive(n, 1, 2)
        group(at_x(-pick(n, (0, 2))), functools.partial(block, late=True), 2)
        return 0

    def rest(n, _):
        group(at_x(-pick(n, (2, 0))), finish, 1)
        leave(n, 0, 2)
        return 0

    lax.fori_loop(0, 2, near, 0)
    lax.fori_loop(0, 2, far, 0)
    z_out_hop(1)
    lax.fori_loop(0, 2, rest, 0)
    for a in (0, 1):
        local_out(a).start()
    for h in range(2, half + 1):
        z_out_hop(h)
    z_out_last()

    for a in range(4):
        local_out(a).wait()
        for r in (1, 2, 3):
            x_out_wait(a, r)
            x_out(a, r).wait_send()
            x_in(a, r).wait_send()
    for d in (0, 1):
        for h in range(1, half + 1):
            for s in range(NX):
                z_in(d, h, s).wait_send()
                z_out(d, h, s).wait_send()


def settle(*refs):
    srcs, dsts, sem = refs[:4], refs[4:8], refs[8]
    copies = [
        pltpu.make_async_copy(src, dst, sem.at[n]) for n, (src, dst) in enumerate(zip(srcs, dsts))
    ]
    for c in copies:
        c.start()
    for c in copies:
        c.wait()


def local(queries, keys, values, output_gradient, doc_lengths, span_order):
    nz = lax.axis_size("ctx") // NX
    half = nz // 2
    rows = queries.shape[0]
    per = rows // C
    blocks = per * NX * nz
    hbm = pl.BlockSpec(memory_space=pl.ANY)
    dma = pltpu.SemaphoreType.DMA
    outs = (
        jax.ShapeDtypeStruct(queries.shape, BF16),
        jax.ShapeDtypeStruct(queries.shape, BF16),
        jax.ShapeDtypeStruct(keys.shape, BF16),
        jax.ShapeDtypeStruct(keys.shape, BF16),
    )
    results = pl.pallas_call(
        functools.partial(kernel, nz),
        out_shape=tuple(pltpu.VMEM(o.shape, o.dtype) for o in outs),
        in_specs=[hbm] * 6,
        out_specs=(pl.BlockSpec(memory_space=pltpu.VMEM),) * 4,
        scratch_shapes=[
            pltpu.VMEM((2, blocks, C, HD), BF16),
            pltpu.VMEM((NX * rows, GW), BF16),
            pltpu.VMEM((NX * rows, GW), BF16),
            pltpu.VMEM((NX * rows, GW), BF16),
            pltpu.VMEM((NX * rows, GW), BF16),
            pltpu.VMEM((NX * per, NB + 2, C, HD), F32),
            pltpu.VMEM((NX * per, NB + 2, C, HD), F32),
            pltpu.VMEM((NX * per, W, GH * C), BF16),
            pltpu.VMEM((NX * per, W, GH * C), BF16),
            pltpu.VMEM((2, half, NX, 2, per, C, HD), BF16),
            pltpu.VMEM((2, half, NX, 2, per, C, HD), BF16),
            pltpu.VMEM((2, NX * rows, HD), BF16),
            pltpu.SMEM(doc_lengths.shape, jnp.int32),
            pltpu.SMEM(span_order.shape, jnp.int32),
            pltpu.VMEM((8, 128), jnp.int32),
            pltpu.SMEM((8, 128), jnp.int32),
            dma((11,)),
            dma((4, 3)),
            dma((4, 3)),
            dma((2, half, NX)),
            dma((2, half, NX)),
            dma((4, 3)),
            dma((4, 3)),
            dma((2, half, NX)),
            dma((2, half, NX)),
        ],
        compiler_params=pltpu.CompilerParams(
            collective_id=0, has_side_effects=True, vmem_limit_bytes=56 * 2**20
        ),
    )(
        queries,
        keys.reshape(per, C, KH * HD),
        values.reshape(per, C, KH * HD),
        output_gradient,
        doc_lengths,
        span_order,
    )
    return pl.pallas_call(
        settle,
        out_shape=outs,
        in_specs=[hbm] * 4,
        out_specs=(hbm,) * 4,
        scratch_shapes=[dma((4,))],
    )(*(pltpu.with_memory_space_constraint(r, pltpu.VMEM) for r in results))


def solution(mesh):
    wide = P(("dp", "ctx"), None)
    return jax.shard_map(
        local,
        mesh=mesh,
        in_specs=(wide, wide, wide, wide, P("dp"), P("dp")),
        out_specs=(wide, wide, wide, wide),
        check_vma=False,
    )
```
